512 devices in a mesh: ctx: 64 (over y_lo, z, core), head: 8 (over x, y_hi).
Axes of the slice: x: 4, y: 4 (y_hi: 2, y_lo: 2; y = y_hi * 2 + y_lo), z: 16, core: 2. Of those that a mesh axis runs over, the one named last changes fastest.
Arguments:
- queries: bfloat16 [65536, 8, 128], P('ctx', 'head'), may hold values from -6 to 6
- keys: bfloat16 [65536, 128], P('ctx'), may hold values from -6 to 6
- values: bfloat16 [65536, 128], P('ctx'), may hold values from -6 to 6
- outputs: bfloat16 [65536, 8, 128], P('ctx', 'head'), may hold values from -6 to 6
- out_grad: bfloat16 [65536, 8, 128], P('ctx', 'head'), may hold values from -16 to 16
- log_norm: float32 [8, 65536], P('head', 'ctx'), may hold values from 6 to 8
- span_ids: int32 [128], replicated, may hold values from 0 to 127, as said below
Outputs:
- query_grad: bfloat16 [65536, 8, 128], P('ctx', 'head')
- key_grad: bfloat16 [65536, 128], P(('ctx', 'head'))
- value_grad: bfloat16 [65536, 128], P(('ctx', 'head'))
The draws below stay inside these ranges and needn't reach their ends.
Inputs may be any that keep to these rules, and one draw needn't show every extreme that they name: `span_ids`: a permutation of 0 to 127 in which blocks 2 k and 2 k + 1 hold two spans that sum to 127.
All inputs are finite; a program needn't handle non-finite values.
Results may differ from the reference program's by a relative error of at most 0.0065.
Values may be sent and summed in bfloat16 or wider, within the bound.
A program may use at most 64 MiB of HBM per device.

```python
import jax
import jax.numpy as jnp
from jax import lax

HEAD_DIM = 128
HEADS = 8
TOK_DEV = 1024
STEPS = 3
TOKENS = 65536
SPANS = 128
SPAN = 512


def draw_span_ids(key, part):
    key = jax.random.fold_in(key, 7)
    half = SPANS // 2
    order = jax.random.permutation(jax.random.fold_in(key, 1), half).astype(jnp.int32)
    flips = jax.random.randint(jax.random.fold_in(key, 2), (half,), 0, 2).astype(jnp.int32)
    lower = order
    upper = (SPANS - 1 - order).astype(jnp.int32)
    first = jnp.where(flips == 1, upper, lower)
    second = jnp.where(flips == 1, lower, upper)
    return jnp.stack([first, second], axis=1).reshape(-1).astype(jnp.int32)


def block_scale(own_key, shape, pieces, low, largest):
    factor_of = 1.0
    for position, shards_of in pieces:
        heights = jax.random.uniform(jax.random.fold_in(jax.random.fold_in(own_key, 6), position), (shards_of,), jnp.float32, low / len(pieces), largest / len(pieces))
        factor_of = factor_of * jnp.repeat(jnp.exp(heights), shape[position] // shards_of).reshape((-1,) + (1,) * (len(shape) - 1 - position))
    return factor_of


def scatter_about(rng, dims, deviation, reach, cuts=(), kind=jnp.bfloat16):
    gain = block_scale(rng, dims, cuts, -0.22, 0.18) if cuts else 1.0
    array = jax.random.normal(rng, dims, jnp.float32) * deviation * gain
    return jnp.minimum(jnp.maximum(array, -reach), reach).astype(kind)


def setup_inputs(seed: int = 0) -> dict:
    streams_of = jax.random.split(jax.random.key(seed), 8)
    queries = scatter_about(streams_of[0], (TOKENS, HEADS, HEAD_DIM), 1.0, 6.0, ((0, 64), (1, 8)))
    keys = scatter_about(streams_of[1], (TOKENS, HEAD_DIM), 1.0, 6.0, ((0, 64),))
    values = scatter_about(streams_of[2], (TOKENS, HEAD_DIM), 1.0, 6.0, ((0, 64),))
    outputs = scatter_about(streams_of[3], (TOKENS, HEADS, HEAD_DIM), 1.0, 6.0, ((0, 64), (1, 8)))
    out_grad = scatter_about(streams_of[4], (TOKENS, HEADS, HEAD_DIM), 4.0, 16.0, ((0, 64), (1, 8)))
    log_norm = jnp.clip(6.0 + 2.0 * jax.random.uniform(streams_of[5], (HEADS, TOKENS), jnp.float32) ** block_scale(streams_of[5], (HEADS, TOKENS), ((0, 8), (1, 64)), -0.2, 0.2), 6.0, 8.0)
    span_ids = draw_span_ids(jax.random.fold_in(streams_of[7], 71), 0)
    return {"queries": queries, "keys": keys, "values": values, "outputs": outputs, "out_grad": out_grad, "log_norm": log_norm, "span_ids": span_ids}


def reference(queries, keys, values, outputs, out_grad, log_norm, span_ids):
    scale = HEAD_DIM ** -0.5
    holders = SPANS // 2
    offsets = jnp.arange(SPAN, dtype=jnp.int32)
    places = (span_ids[:, None] * SPAN + offsets[None, :]).reshape(-1).astype(jnp.int32)
    delta = jnp.sum(out_grad.astype(jnp.float32) * outputs.astype(jnp.float32), axis=2)

    def one_holder(carry, holder):
        key_acc, value_acc = carry
        start = (holder * TOK_DEV).astype(jnp.int32)
        query_rows = lax.dynamic_slice_in_dim(queries, start, TOK_DEV, 0).astype(jnp.float32)
        grad_rows = lax.dynamic_slice_in_dim(out_grad, start, TOK_DEV, 0).astype(jnp.float32)
        norm_rows = lax.dynamic_slice_in_dim(log_norm, start, TOK_DEV, 1)
        delta_rows = lax.dynamic_slice_in_dim(delta, start, TOK_DEV, 0)
        query_places = lax.dynamic_slice_in_dim(places, start, TOK_DEV, 0)
        query_total = jnp.zeros((TOK_DEV, HEADS, HEAD_DIM), jnp.float32)
        for step in range(STEPS):
            source = ((holder - step) % holders).astype(jnp.int32)
            key_start = (source * TOK_DEV).astype(jnp.int32)
            key_rows = lax.dynamic_slice_in_dim(keys, key_start, TOK_DEV, 0).astype(jnp.float32)
            value_rows = lax.dynamic_slice_in_dim(values, key_start, TOK_DEV, 0).astype(jnp.float32)
            key_places = lax.dynamic_slice_in_dim(places, key_start, TOK_DEV, 0)
            allowed = key_places[None, :] <= query_places[:, None]
            scores = jnp.einsum('qhd,kd->hqk', query_rows, key_rows) * scale
            prob = jnp.where(allowed[None], jnp.exp(scores - norm_rows[:, :, None]), 0.0)
            prob16 = lax.optimization_barrier(prob.astype(jnp.bfloat16)).astype(jnp.float32)
            value_part = jnp.einsum('hqk,qhd->kd', prob16, grad_rows)
            dprob = jnp.einsum('qhd,kd->hqk', grad_rows, value_rows)
            dscore = lax.optimization_barrier((prob * (dprob - delta_rows.T[:, :, None])).astype(jnp.bfloat16)).astype(jnp.float32)
            query_total = query_total + scale * jnp.einsum('hqk,kd->qhd', dscore, key_rows)
            key_part = scale * jnp.einsum('hqk,qhd->kd', dscore, query_rows)
            old_key = lax.dynamic_slice_in_dim(key_acc, key_start, TOK_DEV, 0)
            key_acc = lax.dynamic_update_slice_in_dim(key_acc, old_key + key_part, key_start, 0)
            old_value = lax.dynamic_slice_in_dim(value_acc, key_start, TOK_DEV, 0)
            value_acc = lax.dynamic_update_slice_in_dim(value_acc, old_value + value_part, key_start, 0)
        return (key_acc, value_acc), query_total.astype(jnp.bfloat16)

    zeros = jnp.zeros((TOKENS, HEAD_DIM), jnp.float32)
    (key_acc, value_acc), query_parts = lax.scan(one_holder, (zeros, zeros), jnp.arange(holders, dtype=jnp.int32))
    query_grad = query_parts.reshape(TOKENS, HEADS, HEAD_DIM)
    return query_grad, key_acc.astype(jnp.bfloat16), value_acc.astype(jnp.bfloat16)
```

```python
import jax
import jax.numpy as jnp
from jax import lax
from jax.experimental import pallas as pl
from jax.experimental.pallas import tpu as pltpu
from jax.sharding import PartitionSpec as P

MESH = pl.DeviceIdType.MESH
F32 = jnp.float32
BF16 = jnp.bfloat16
LOG2E = 1.4426950408889634
NT = (((1,), (1,)), ((), ()))
TN = (((0,), (0,)), ((), ()))
SPAN = 512
TOK = 2 * SPAN
DIM = 128
SCALE = DIM ** -0.5


def tile(q, g, norm, delta, k, v, diagonal=False):
    score = lax.dot_general(k, q, NT, preferred_element_type=F32)
    prob = jnp.exp2(score * (SCALE * LOG2E) - norm)
    if diagonal:
        rows = lax.broadcasted_iota(jnp.int32, score.shape, 0)
        prob = jnp.where(rows <= lax.broadcasted_iota(jnp.int32, score.shape, 1), prob, 0.0)
    dprob = lax.dot_general(v, g, NT, preferred_element_type=F32)
    dscore = (prob * (dprob - delta)).astype(BF16)
    dv = jnp.dot(prob.astype(BF16), g, preferred_element_type=F32)
    dk = jnp.dot(dscore, q, preferred_element_type=F32)
    dq = lax.dot_general(dscore, k, TN, preferred_element_type=F32)
    return dq, dk, dv


def kernel(
    holders, heads, span_ref, q_in, g_in, o_in, k_in, v_in, norm_in, dq_out, dk_out, dv_out,
    raw_q, raw_g, raw_k, raw_v, raw_o, q_own, q_far, kv_own, kv_mate, kv_far,
    norm_own, norm_far, delta_own, delta_far, dq_acc, dk_acc, dv_acc, dq_end, dk_end, dv_end,
    mate_out, mate_part, next_out, dq_part, back_out, back_part, own_out, own_part,
    load_sem, kv_sem, mate_sem, far_sem, row_sem, dq_sem, back_send, back_recv, own_send, own_recv, ready,
):
    c = lax.axis_index("ctx")
    h = lax.axis_index("head")
    side = lax.rem(c, 2)
    even, odd = side == 0, side == 1
    mate = {"ctx": c + 1 - 2 * side}
    ahead = lax.rem(c + 2, holders)
    behind = lax.rem(c + holders - 2, holders)

    loads = [
        pltpu.make_async_copy(ref, raw, load_sem.at[i])
        for i, (ref, raw) in enumerate(
            ((q_in, raw_q), (g_in, raw_g), (k_in, raw_k), (v_in, raw_v), (o_in, raw_o))
        )
    ]
    for copy in loads:
        copy.start()

    barrier = pltpu.get_barrier_semaphore()
    pl.semaphore_signal(barrier, inc=1, device_id=mate, device_id_type=MESH)
    pl.semaphore_signal(barrier, inc=1, device_id={"ctx": behind}, device_id_type=MESH)
    for step in range(1, heads):
        pl.semaphore_signal(
            barrier, inc=1, device_id={"head": lax.rem(h + step, heads)}, device_id_type=MESH
        )

    def first(holder):
        return span_ref[2 * holder]

    def second(holder):
        return span_ref[2 * holder + 1]

    def low_span(holder):
        return jnp.minimum(first(holder), second(holder))

    def late(holder):
        return (first(holder) > second(holder)).astype(jnp.int32)

    low_place = late(c)
    asks = jnp.where(even, ahead, c)
    lows = [
        (low_span(c + 1 - 2 * side) < low_span(asks)).astype(jnp.int32),
        (low_span(jnp.where(even, c, behind)) < low_span(asks)).astype(jnp.int32),
    ]

    lo, hi = low_place * SPAN, (1 - low_place) * SPAN
    for copy in loads[:4]:
        copy.wait()
    for i, (raw, place) in enumerate(((raw_q, hi), (raw_g, hi), (raw_q, lo), (raw_g, lo))):
        q_own[pl.ds(i * SPAN, SPAN)] = raw[pl.ds(place, SPAN)]
    for i, (raw, place) in enumerate(((raw_k, lo), (raw_v, lo), (raw_k, hi), (raw_v, hi))):
        kv_own[pl.ds(i * SPAN, SPAN)] = raw[pl.ds(place, SPAN)]
    loads[4].wait()
    for i, place in enumerate((hi, lo)):
        norm_own[:, pl.ds(i * SPAN, SPAN)] = norm_in[:, pl.ds(place, SPAN)] * LOG2E
        product = raw_g[pl.ds(place, SPAN)].astype(F32) * raw_o[pl.ds(place, SPAN)].astype(F32)
        delta_own[:, pl.ds(i * SPAN, SPAN)] = jnp.sum(product.T, axis=0, keepdims=True)

    pl.semaphore_wait(barrier, heads + 1)

    def remote(src, dst, send, recv, device):
        return pltpu.make_async_remote_copy(
            src_ref=src, dst_ref=dst, send_sem=send, recv_sem=recv, device_id=device, device_id_type=MESH
        )

    half = lambda i: pl.ds(i * TOK, TOK)
    kv_copy = remote(kv_own, kv_mate, kv_sem.at[0], kv_sem.at[1], mate)
    q_copies = [
        remote(q_own.at[half(i)], q_far.at[half(i)], far_sem.at[0, i], far_sem.at[1, i], {"ctx": behind})
        for i in range(2)
    ]
    row_copies = [
        remote(own, far, row_sem.at[0, i], row_sem.at[1, i], {"ctx": behind})
        for i, (own, far) in enumerate(((norm_own, norm_far), (delta_own, delta_far)))
    ]
    back_copies = [
        remote(kv_own.at[half(i)], kv_far.at[half(i)], far_sem.at[0, i], far_sem.at[1, i], {"ctx": ahead})
        for i in range(2)
    ]

    kv_copy.start()

    @pl.when(odd)
    def _():
        for copy in back_copies:
            copy.start()

    @pl.when(even)
    def _():
        pl.semaphore_signal(ready, inc=1, device_id={"ctx": ahead}, device_id_type=MESH)
        pl.semaphore_wait(ready, 1)
        for copy in (*row_copies, *q_copies):
            copy.start()

    def either(a, b):
        return a + b - 2 * a * b

    def at(i, size):
        return pl.ds(i * size, size)

    def block(qslot, qpart, kvslot, kvpart, diagonal=False):
        q, norm, delta = ((q_own, norm_own, delta_own), (q_far, norm_far, delta_far))[qslot]
        kv = (kv_own, kv_mate, kv_far)[kvslot]
        return tile(
            q[at(2 * qpart, SPAN)],
            q[at(2 * qpart + 1, SPAN)],
            norm[:, at(qpart, SPAN)],
            delta[:, at(qpart, SPAN)],
            kv[at(2 * kvpart, SPAN)],
            kv[at(2 * kvpart + 1, SPAN)],
            diagonal,
        )

    def crossing(qslot, kvslot, new_q, new_kv):
        dq, dk, dv = block(qslot, 0, kvslot, 0)
        top = pl.ds(0, SPAN)
        dq_acc[qslot, top] = dq if new_q else dq_acc[qslot, top] + dq
        dk_acc[kvslot, top] = dk if new_kv else dk_acc[kvslot, top] + dk
        dv_acc[kvslot, top] = dv if new_kv else dv_acc[kvslot, top] + dv

    def level(pair, qslot, kvslot):
        dq, dk, dv = block(qslot, lows[pair], kvslot, 1 - lows[pair])
        top = pl.ds(0, SPAN)
        dq_end[pair, top] = dq
        dk_end[pair, top] = dk
        dv_end[pair, top] = dv

    crossing(0, 0, True, True)
    dq, dk, dv = block(0, 1, 0, 0, True)
    dq_acc[0, pl.ds(SPAN, SPAN)] = dq
    dk_acc[0, pl.ds(0, SPAN)] += dk
    dv_acc[0, pl.ds(0, SPAN)] += dv
    dq, dk, dv = block(0, 0, 0, 1, True)
    dq_acc[0, pl.ds(0, SPAN)] += dq
    dk_acc[0, pl.ds(SPAN, SPAN)] = dk
    dv_acc[0, pl.ds(SPAN, SPAN)] = dv

    for ref in (dk_acc, dv_acc):
        for slot in (1, 2):
            ref[slot, pl.ds(SPAN, SPAN)] = jnp.zeros((SPAN, DIM), F32)
    for ref in (dq_end, dk_end, dv_end):
        for pair in range(2):
            ref[pair, pl.ds(SPAN, SPAN)] = jnp.zeros((SPAN, DIM), F32)

    def if_low(pair, part, end, on=1):
        return end[pair, at(1 - on * either(lows[pair], part), SPAN)]

    mate_copy = remote(mate_out, mate_part, mate_sem.at[0], mate_sem.at[1], mate)

    def send_mate():
        for part in range(2):
            for i, (acc, end, factor) in enumerate(((dk_acc, dk_end, SCALE), (dv_acc, dv_end, 1.0))):
                value = if_low(0, part, end)
                if part == 0:
                    value += acc[1, pl.ds(0, SPAN)]
                mate_out[pl.ds(part * TOK + i * SPAN, SPAN)] = (value * factor).astype(BF16)
        mate_copy.start()

    dq_copy = remote(next_out, dq_part, dq_sem.at[0], dq_sem.at[1], {"ctx": ahead})
    back_sends = [
        remote(
            back_out.at[to], back_part.at[h], back_send.at[to], back_recv.at[h], {"ctx": behind, "head": to}
        )
        for to in range(heads)
    ]

    @pl.when(even)
    def _():
        kv_copy.wait_recv()
        for copy in row_copies:
            copy.wait_recv()
        q_copies[0].wait_recv()
        crossing(1, 1, True, True)
        crossing(1, 0, False, False)
        q_copies[1].wait_recv()
        level(0, 1, 1)
        send_mate()
        level(1, 1, 0)
        for part in range(2):
            value = if_low(0, 1 - part, dq_end) + if_low(1, 1 - part, dq_end)
            if part == 0:
                value += dq_acc[1, pl.ds(0, SPAN)]
            next_out[pl.ds(part * SPAN, SPAN)] = (value * SCALE).astype(BF16)
        dq_copy.start()

    low_of = [low_place, 1 - low_place]

    @pl.when(odd)
    def _():
        kv_copy.wait_recv()
        crossing(0, 1, False, True)
        level(0, 0, 1)
        send_mate()
        back_copies[0].wait_recv()
        crossing(0, 2, False, True)
        back_copies[1].wait_recv()
        level(1, 0, 2)
        place = late(behind)
        for p in range(2):
            part = either(place, p)
            for i, (acc, end, factor) in enumerate(((dk_acc, dk_end, SCALE), (dv_acc, dv_end, 1.0))):
                value = if_low(1, part, end) + acc[2, at(part, SPAN)]
                value = (value * factor).astype(BF16)
                each = TOK // heads
                for s in range(heads // 2):
                    back_out[p * (heads // 2) + s, pl.ds(i * each, each)] = value[s * each : (s + 1) * each]
        for copy in back_sends:
            copy.start()

    mate_copy.wait_recv()
    each = TOK // heads
    for p in range(2):
        part = low_of[p]
        for i, (acc, end, factor) in enumerate(((dk_acc, dk_end, SCALE), (dv_acc, dv_end, 1.0))):
            value = (acc[0, at(part, SPAN)] + if_low(1, part, end, 1 - side)) * factor
            value += mate_part[at(2 * part + i, SPAN)].astype(F32)
            value = value.astype(BF16)
            for s in range(heads // 2):
                own_out[p * (heads // 2) + s, pl.ds(i * each, each)] = value[s * each : (s + 1) * each]
    own_sends = []
    for step in range(1, heads):
        to = lax.rem(h + step, heads)
        own_sends.append(remote(own_out.at[to], own_part.at[h], own_send.at[to], own_recv.at[h], {"head": to}))
        own_sends[-1].start()
    own_part[h] = own_out[h]

    @pl.when(even)
    def _():
        dq_copy.wait_recv()
        for p in range(2):
            place = (1 - low_of[p]) * SPAN
            value = dq_acc[0, pl.ds(place, SPAN)] * SCALE + dq_part[pl.ds(place, SPAN)].astype(F32)
            dq_out[pl.ds(p * SPAN, SPAN)] = value.astype(BF16)

    @pl.when(odd)
    def _():
        for p in range(2):
            place = (1 - low_of[p]) * SPAN
            value = dq_acc[0, pl.ds(place, SPAN)]
            value += if_low(0, low_of[p], dq_end) + if_low(1, low_of[p], dq_end)
            dq_out[pl.ds(p * SPAN, SPAN)] = (value * SCALE).astype(BF16)

    for step in range(1, heads):
        sender = lax.rem(h + step, heads)
        remote(own_out.at[sender], own_part.at[sender], own_send.at[sender], own_recv.at[sender], mate).wait_recv()
    total = own_part[0].astype(F32)
    for i in range(1, heads):
        total += own_part[i].astype(F32)
    dk_out[...] = total[:each].astype(BF16)
    dv_out[...] = total[each:].astype(BF16)

    @pl.when(odd)
    def _():
        for i in range(heads):
            remote(back_out.at[i], back_part.at[i], back_send.at[i], back_recv.at[i], mate).wait_recv()
        more = total
        for i in range(heads):
            more += back_part[i].astype(F32)
        dk_out[...] = more[:each].astype(BF16)
        dv_out[...] = more[each:].astype(BF16)

    kv_copy.wait_send()
    mate_copy.wait_send()
    for copy in own_sends:
        copy.wait_send()

    @pl.when(even)
    def _():
        for copy in (*row_copies, *q_copies, dq_copy):
            copy.wait_send()

    @pl.when(odd)
    def _():
        for copy in (*back_copies, *back_sends):
            copy.wait_send()


def local(queries, keys, values, outputs, out_grad, log_norm, span_ids):
    holders, heads = lax.axis_size("ctx"), lax.axis_size("head")
    each = TOK // heads
    flat = lambda a: a.reshape(TOK, DIM)
    body = lambda *refs: kernel(holders, heads, *refs)
    dma = pltpu.SemaphoreType.DMA
    dq, dk, dv = pl.pallas_call(
        body,
        out_shape=[
            jax.ShapeDtypeStruct((TOK, DIM), BF16),
            jax.ShapeDtypeStruct((each, DIM), BF16),
            jax.ShapeDtypeStruct((each, DIM), BF16),
        ],
        in_specs=[
            pl.BlockSpec(memory_space=pltpu.SMEM),
            *[pl.BlockSpec(memory_space=pl.ANY)] * 5,
            pl.BlockSpec(memory_space=pltpu.VMEM),
        ],
        out_specs=[pl.BlockSpec(memory_space=pltpu.VMEM)] * 3,
        scratch_shapes=[
            *[pltpu.VMEM((TOK, DIM), BF16)] * 5,
            *[pltpu.VMEM((2 * TOK, DIM), BF16)] * 5,
            *[pltpu.VMEM((1, TOK), F32)] * 4,
            pltpu.VMEM((2, TOK, DIM), F32),
            pltpu.VMEM((3, TOK, DIM), F32),
            pltpu.VMEM((3, TOK, DIM), F32),
            pltpu.VMEM((2, TOK, DIM), F32),
            pltpu.VMEM((2, TOK, DIM), F32),
            pltpu.VMEM((2, TOK, DIM), F32),
            pltpu.VMEM((2 * TOK, DIM), BF16),
            pltpu.VMEM((2 * TOK, DIM), BF16),
            pltpu.VMEM((TOK, DIM), BF16),
            pltpu.VMEM((TOK, DIM), BF16),
            pltpu.VMEM((heads, 2 * each, DIM), BF16),
            pltpu.VMEM((heads, 2 * each, DIM), BF16),
            pltpu.VMEM((heads, 2 * each, DIM), BF16),
            pltpu.VMEM((heads, 2 * each, DIM), BF16),
            dma((5,)),
            dma((2,)),
            dma((2,)),
            dma((2, 2)),
            dma((2, 2)),
            dma((2,)),
            dma((heads,)),
            dma((heads,)),
            dma((heads,)),
            dma((heads,)),
            pltpu.SemaphoreType.REGULAR,
        ],
        compiler_params=pltpu.CompilerParams(
            collective_id=0, has_side_effects=True, vmem_limit_bytes=40 * 1024 * 1024
        ),
    )(
        span_ids,
        flat(queries),
        flat(out_grad),
        flat(outputs),
        keys,
        values,
        log_norm,
    )
    return dq.reshape(queries.shape), dk, dv


def solution(mesh):
    in_specs = (
        P("ctx", "head", None),
        P("ctx", None),
        P("ctx", None),
        P("ctx", "head", None),
        P("ctx", "head", None),
        P("head", "ctx"),
        P(),
    )
    out_specs = (P("ctx", "head", None), P(("ctx", "head"), None), P(("ctx", "head"), None))
    return jax.shard_map(local, mesh=mesh, in_specs=in_specs, out_specs=out_specs, check_vma=False)
```

```python
import jax
import jax.numpy as jnp
from jax import lax
from jax.experimental import pallas as pl
from jax.experimental.pallas import tpu as pltpu
from jax.sharding import PartitionSpec as P

MESH = pl.DeviceIdType.MESH
F32 = jnp.float32
BF16 = jnp.bfloat16
LOG2E = 1.4426950408889634
NT = (((1,), (1,)), ((), ()))
TN = (((0,), (0,)), ((), ()))
SPAN = 512
LINE = 16
VMEM_GRANT = 63 * 1024 * 1024
TOK = 2 * SPAN
DIM = 128
SCALE = DIM ** -0.5


def tile(q, g, norm, delta, k, v, diagonal=False):
    score = lax.dot_general(k, q, NT, preferred_element_type=F32)
    prob = jnp.exp2(score * (SCALE * LOG2E) - norm)
    if diagonal:
        rows = lax.broadcasted_iota(jnp.int32, score.shape, 0)
        prob = jnp.where(rows <= lax.broadcasted_iota(jnp.int32, score.shape, 1), prob, 0.0)
    dprob = lax.dot_general(v, g, NT, preferred_element_type=F32)
    dscore = (prob * (dprob - delta)).astype(BF16)
    dv = jnp.dot(prob.astype(BF16), g, preferred_element_type=F32)
    dk = jnp.dot(dscore, q, preferred_element_type=F32)
    dq = lax.dot_general(dscore, k, TN, preferred_element_type=F32)
    return dq, dk, dv


def kernel(
    holders, heads, span_in, q_in, g_in, o_in, k_in, v_in, norm_in, dq_out, dk_out, dv_out,
    span_ref, raw_norm, raw_q, raw_g, raw_k, raw_v, raw_o, q_own, q_far, kv_own, kv_mate, kv_far,
    norm_own, norm_far, delta_own, delta_far, dq_acc, dk_acc, dv_acc, dq_end, dk_end, dv_end,
    mate_out, mate_part, next_out, dq_part, back_out, back_part, own_out, own_part,
    load_sem, kv_sem, mate_sem, far_sem, row_sem, dq_sem, back_send, back_recv, own_send, own_recv, ready,
):
    c = lax.axis_index("ctx")
    h = lax.axis_index("head")
    side = lax.rem(c, 2)
    even, odd = side == 0, side == 1
    mate = {"ctx": c + 1 - 2 * side}
    ahead = lax.rem(c + 2, holders)
    behind = lax.rem(c + holders - 2, holders)

    place_in_line = lax.rem(lax.div(c, 2), LINE)
    start_of_line, last = place_in_line == 0, place_in_line == LINE - 1

    loads = [
        pltpu.make_async_copy(ref, raw, load_sem.at[i])
        for i, (ref, raw) in enumerate(
            (
                (span_in, span_ref), (k_in, raw_k), (v_in, raw_v), (q_in, raw_q), (g_in, raw_g),
                (norm_in, raw_norm), (o_in, raw_o),
            )
        )
    ]
    for copy in loads:
        copy.start()

    barrier = pltpu.get_barrier_semaphore()
    pl.semaphore_signal(barrier, inc=1, device_id=mate, device_id_type=MESH)
    pl.semaphore_signal(barrier, inc=1, device_id={"ctx": behind}, device_id_type=MESH)

    @pl.when(jnp.logical_not(last))
    def _():
        pl.semaphore_signal(barrier, inc=1, device_id={"ctx": ahead}, device_id_type=MESH)

    for step in range(1, heads):
        pl.semaphore_signal(
            barrier, inc=1, device_id={"head": lax.rem(h + step, heads)}, device_id_type=MESH
        )

    loads[0].wait()

    def first(holder):
        return span_ref[2 * holder]

    def second(holder):
        return span_ref[2 * holder + 1]

    def low_span(holder):
        return jnp.minimum(first(holder), second(holder))

    def late(holder):
        return (first(holder) > second(holder)).astype(jnp.int32)

    low_place = late(c)
    asks = jnp.where(even, ahead, c)
    lows = [
        (low_span(c + 1 - 2 * side) < low_span(asks)).astype(jnp.int32),
        (low_span(jnp.where(even, c, behind)) < low_span(asks)).astype(jnp.int32),
    ]

    lo, hi = low_place * SPAN, (1 - low_place) * SPAN
    for copy in loads[1:5]:
        copy.wait()
    for i, (raw, place) in enumerate(((raw_q, hi), (raw_g, hi), (raw_q, lo), (raw_g, lo))):
        q_own[pl.ds(i * SPAN, SPAN)] = raw[pl.ds(place, SPAN)]
    for i, (raw, place) in enumerate(((raw_k, lo), (raw_v, lo), (raw_k, hi), (raw_v, hi))):
        kv_own[pl.ds(i * SPAN, SPAN)] = raw[pl.ds(place, SPAN)]
    for copy in loads[5:]:
        copy.wait()
    for i, place in enumerate((hi, lo)):
        norm_own[:, pl.ds(i * SPAN, SPAN)] = raw_norm[:, pl.ds(place, SPAN)] * LOG2E
        product = raw_g[pl.ds(place, SPAN)].astype(F32) * raw_o[pl.ds(place, SPAN)].astype(F32)
        delta_own[:, pl.ds(i * SPAN, SPAN)] = jnp.sum(product.T, axis=0, keepdims=True)

    pl.semaphore_wait(barrier, jnp.where(start_of_line, heads + 1, heads + 2))

    @pl.when(last)
    def _():
        pl.semaphore_signal(ready, inc=1, device_id={"ctx": ahead}, device_id_type=MESH)


    def remote(src, dst, send, recv, device):
        return pltpu.make_async_remote_copy(
            src_ref=src, dst_ref=dst, send_sem=send, recv_sem=recv, device_id=device, device_id_type=MESH
        )

    half = lambda i: pl.ds(i * TOK, TOK)
    kv_copy = remote(kv_own, kv_mate, kv_sem.at[0], kv_sem.at[1], mate)
    q_copies = [
        remote(q_own.at[half(i)], q_far.at[half(i)], far_sem.at[0, i], far_sem.at[1, i], {"ctx": behind})
        for i in range(2)
    ]
    row_copies = [
        remote(own, far, row_sem.at[0, i], row_sem.at[1, i], {"ctx": behind})
        for i, (own, far) in enumerate(((norm_own, norm_far), (delta_own, delta_far)))
    ]
    back_copies = [
        remote(kv_own.at[half(i)], kv_far.at[half(i)], far_sem.at[0, i], far_sem.at[1, i], {"ctx": ahead})
        for i in range(2)
    ]

    kv_copy.start()

    @pl.when(odd)
    def _():
        for copy in back_copies:
            copy.start()

    def send_queries():
        for copy in (*row_copies, *q_copies):
            copy.start()

    pl.when(jnp.logical_and(even, jnp.logical_not(start_of_line)))(send_queries)

    def either(a, b):
        return a + b - 2 * a * b

    def at(i, size):
        return pl.ds(i * size, size)

    def block(qslot, qpart, kvslot, kvpart, diagonal=False):
        q, norm, delta = ((q_own, norm_own, delta_own), (q_far, norm_far, delta_far))[qslot]
        kv = (kv_own, kv_mate, kv_far)[kvslot]
        return tile(
            q[at(2 * qpart, SPAN)],
            q[at(2 * qpart + 1, SPAN)],
            norm[:, at(qpart, SPAN)],
            delta[:, at(qpart, SPAN)],
            kv[at(2 * kvpart, SPAN)],
            kv[at(2 * kvpart + 1, SPAN)],
            diagonal,
        )

    def crossing(qslot, kvslot, new_q, new_kv):
        dq, dk, dv = block(qslot, 0, kvslot, 0)
        top = pl.ds(0, SPAN)
        dq_acc[qslot, top] = dq if new_q else dq_acc[qslot, top] + dq
        dk_acc[kvslot, top] = dk if new_kv else dk_acc[kvslot, top] + dk
        dv_acc[kvslot, top] = dv if new_kv else dv_acc[kvslot, top] + dv

    def level(pair, qslot, kvslot):
        dq, dk, dv = block(qslot, lows[pair], kvslot, 1 - lows[pair])
        top = pl.ds(0, SPAN)
        dq_end[pair, top] = dq
        dk_end[pair, top] = dk
        dv_end[pair, top] = dv

    crossing(0, 0, True, True)
    dq, dk, dv = block(0, 1, 0, 0, True)
    dq_acc[0, pl.ds(SPAN, SPAN)] = dq
    dk_acc[0, pl.ds(0, SPAN)] += dk
    dv_acc[0, pl.ds(0, SPAN)] += dv
    dq, dk, dv = block(0, 0, 0, 1, True)
    dq_acc[0, pl.ds(0, SPAN)] += dq
    dk_acc[0, pl.ds(SPAN, SPAN)] = dk
    dv_acc[0, pl.ds(SPAN, SPAN)] = dv

    @pl.when(start_of_line)
    def _():
        pl.semaphore_wait(ready, 1)

    pl.when(jnp.logical_and(even, start_of_line))(send_queries)

    for ref in (dk_acc, dv_acc):
        for slot in (1, 2):
            ref[slot, pl.ds(SPAN, SPAN)] = jnp.zeros((SPAN, DIM), F32)
    for ref in (dq_end, dk_end, dv_end):
        for pair in range(2):
            ref[pair, pl.ds(SPAN, SPAN)] = jnp.zeros((SPAN, DIM), F32)

    def if_low(pair, part, end, on=1):
        return end[pair, at(1 - on * either(lows[pair], part), SPAN)]

    mate_copy = remote(mate_out, mate_part, mate_sem.at[0], mate_sem.at[1], mate)

    def send_mate():
        for part in range(2):
            for i, (acc, end, factor) in enumerate(((dk_acc, dk_end, SCALE), (dv_acc, dv_end, 1.0))):
                value = if_low(0, part, end)
                if part == 0:
                    value += acc[1, pl.ds(0, SPAN)]
                mate_out[pl.ds(part * TOK + i * SPAN, SPAN)] = (value * factor).astype(BF16)
        mate_copy.start()

    dq_copy = remote(next_out, dq_part, dq_sem.at[0], dq_sem.at[1], {"ctx": ahead})
    back_sends = [
        remote(
            back_out.at[to], back_part.at[h], back_send.at[to], back_recv.at[h], {"ctx": behind, "head": to}
        )
        for to in range(heads)
    ]

    @pl.when(even)
    def _():
        kv_copy.wait_recv()
        for copy in row_copies:
            copy.wait_recv()
        q_copies[0].wait_recv()
        crossing(1, 1, True, True)
        crossing(1, 0, False, False)
        q_copies[1].wait_recv()
        level(0, 1, 1)
        send_mate()
        level(1, 1, 0)
        for part in range(2):
            value = if_low(0, 1 - part, dq_end) + if_low(1, 1 - part, dq_end)
            if part == 0:
                value += dq_acc[1, pl.ds(0, SPAN)]
            next_out[pl.ds(part * SPAN, SPAN)] = (value * SCALE).astype(BF16)
        dq_copy.start()

    low_of = [low_place, 1 - low_place]

    def visit_behind():
        back_copies[0].wait_recv()
        crossing(0, 2, False, True)
        back_copies[1].wait_recv()
        level(1, 0, 2)
        place = late(behind)
        for p in range(2):
            part = either(place, p)
            for i, (acc, end, factor) in enumerate(((dk_acc, dk_end, SCALE), (dv_acc, dv_end, 1.0))):
                value = if_low(1, part, end) + acc[2, at(part, SPAN)]
                value = (value * factor).astype(BF16)
                each = TOK // heads
                for s in range(heads // 2):
                    back_out[p * (heads // 2) + s, pl.ds(i * each, each)] = value[s * each : (s + 1) * each]
        for copy in back_sends:
            copy.start()

    @pl.when(odd)
    def _():
        kv_copy.wait_recv()
        crossing(0, 1, False, True)
        level(0, 0, 1)
        send_mate()

    pl.when(jnp.logical_and(odd, jnp.logical_not(start_of_line)))(visit_behind)

    mate_copy.wait_recv()
    each = TOK // heads
    for p in range(2):
        part = low_of[p]
        for i, (acc, end, factor) in enumerate(((dk_acc, dk_end, SCALE), (dv_acc, dv_end, 1.0))):
            value = (acc[0, at(part, SPAN)] + if_low(1, part, end, 1 - side)) * factor
            value += mate_part[at(2 * part + i, SPAN)].astype(F32)
            value = value.astype(BF16)
            for s in range(heads // 2):
                own_out[p * (heads // 2) + s, pl.ds(i * each, each)] = value[s * each : (s + 1) * each]
    own_sends = []
    for step in range(1, heads):
        to = lax.rem(h + step, heads)
        own_sends.append(remote(own_out.at[to], own_part.at[h], own_send.at[to], own_recv.at[h], {"head": to}))
        own_sends[-1].start()
    own_part[h] = own_out[h]

    pl.when(jnp.logical_and(odd, start_of_line))(visit_behind)

    @pl.when(even)
    def _():
        dq_copy.wait_recv()
        for p in range(2):
            place = (1 - low_of[p]) * SPAN
            value = dq_acc[0, pl.ds(place, SPAN)] * SCALE + dq_part[pl.ds(place, SPAN)].astype(F32)
            dq_out[pl.ds(p * SPAN, SPAN)] = value.astype(BF16)

    @pl.when(odd)
    def _():
        for p in range(2):
            place = (1 - low_of[p]) * SPAN
            value = dq_acc[0, pl.ds(place, SPAN)]
            value += if_low(0, low_of[p], dq_end) + if_low(1, low_of[p], dq_end)
            dq_out[pl.ds(p * SPAN, SPAN)] = (value * SCALE).astype(BF16)

    for step in range(1, heads):
        sender = lax.rem(h + step, heads)
        remote(own_out.at[sender], own_part.at[sender], own_send.at[sender], own_recv.at[sender], mate).wait_recv()
    total = own_part[0].astype(F32)
    for i in range(1, heads):
        total += own_part[i].astype(F32)
    dk_out[...] = total[:each].astype(BF16)
    dv_out[...] = total[each:].astype(BF16)

    @pl.when(odd)
    def _():
        for i in range(heads):
            remote(back_out.at[i], back_part.at[i], back_send.at[i], back_recv.at[i], mate).wait_recv()
        more = total
        for i in range(heads):
            more += back_part[i].astype(F32)
        dk_out[...] = more[:each].astype(BF16)
        dv_out[...] = more[each:].astype(BF16)

    kv_copy.wait_send()
    mate_copy.wait_send()
    for copy in own_sends:
        copy.wait_send()

    @pl.when(even)
    def _():
        for copy in (*row_copies, *q_copies, dq_copy):
            copy.wait_send()

    @pl.when(odd)
    def _():
        for copy in (*back_copies, *back_sends):
            copy.wait_send()


def store(dq, dk, dv, dq_out, dk_out, dv_out, sem):
    copies = [
        pltpu.make_async_copy(src, dst, sem.at[i])
        for i, (src, dst) in enumerate(((dq, dq_out), (dk, dk_out), (dv, dv_out)))
    ]
    for copy in copies:
        copy.start()
    for copy in copies:
        copy.wait()


def local(queries, keys, values, outputs, out_grad, log_norm, span_ids):
    holders, heads = lax.axis_size("ctx"), lax.axis_size("head")
    each = TOK // heads
    flat = lambda a: a.reshape(TOK, DIM)
    body = lambda *refs: kernel(holders, heads, *refs)
    dma = pltpu.SemaphoreType.DMA
    dq, dk, dv = pl.pallas_call(
        body,
        out_shape=[
            jax.ShapeDtypeStruct((TOK, DIM), BF16),
            jax.ShapeDtypeStruct((each, DIM), BF16),
            jax.ShapeDtypeStruct((each, DIM), BF16),
        ],
        in_specs=[
            *[pl.BlockSpec(memory_space=pltpu.HBM)] * 7,
        ],
        out_specs=[pl.BlockSpec(memory_space=pltpu.VMEM)] * 3,
        scratch_shapes=[
            pltpu.SMEM((2 * holders,), jnp.int32),
            pltpu.VMEM((1, TOK), F32),
            *[pltpu.VMEM((TOK, DIM), BF16)] * 5,
            *[pltpu.VMEM((2 * TOK, DIM), BF16)] * 5,
            *[pltpu.VMEM((1, TOK), F32)] * 4,
            pltpu.VMEM((2, TOK, DIM), F32),
            pltpu.VMEM((3, TOK, DIM), F32),
            pltpu.VMEM((3, TOK, DIM), F32),
            pltpu.VMEM((2, TOK, DIM), F32),
            pltpu.VMEM((2, TOK, DIM), F32),
            pltpu.VMEM((2, TOK, DIM), F32),
            pltpu.VMEM((2 * TOK, DIM), BF16),
            pltpu.VMEM((2 * TOK, DIM), BF16),
            pltpu.VMEM((TOK, DIM), BF16),
            pltpu.VMEM((TOK, DIM), BF16),
            pltpu.VMEM((heads, 2 * each, DIM), BF16),
            pltpu.VMEM((heads, 2 * each, DIM), BF16),
            pltpu.VMEM((heads, 2 * each, DIM), BF16),
            pltpu.VMEM((heads, 2 * each, DIM), BF16),
            dma((7,)),
            dma((2,)),
            dma((2,)),
            dma((2, 2)),
            dma((2, 2)),
            dma((2,)),
            dma((heads,)),
            dma((heads,)),
            dma((heads,)),
            dma((heads,)),
            pltpu.SemaphoreType.REGULAR,
        ],
        compiler_params=pltpu.CompilerParams(
            collective_id=0, has_side_effects=True, vmem_limit_bytes=VMEM_GRANT
        ),
    )(
        span_ids,
        flat(queries),
        flat(out_grad),
        flat(outputs),
        keys,
        values,
        log_norm,
    )
    dq, dk, dv = pl.pallas_call(
        store,
        out_shape=[jax.ShapeDtypeStruct(a.shape, BF16) for a in (dq, dk, dv)],
        in_specs=[pl.BlockSpec(memory_space=pltpu.VMEM)] * 3,
        out_specs=[pl.BlockSpec(memory_space=pltpu.HBM)] * 3,
        scratch_shapes=[dma((3,))],
    )(dq, dk, dv)
    return dq.reshape(queries.shape), dk, dv


def solution(mesh):
    in_specs = (
        P("ctx", "head", None),
        P("ctx", None),
        P("ctx", None),
        P("ctx", "head", None),
        P("ctx", "head", None),
        P("head", "ctx"),
        P(),
    )
    out_specs = (P("ctx", "head", None), P(("ctx", "head"), None), P(("ctx", "head"), None))
    return jax.shard_map(local, mesh=mesh, in_specs=in_specs, out_specs=out_specs, check_vma=False)
```

```python
import jax
import jax.numpy as jnp
from jax import lax
from jax.experimental import pallas as pl
from jax.experimental.pallas import tpu as pltpu
from jax.sharding import PartitionSpec as P

MESH = pl.DeviceIdType.MESH
F32 = jnp.float32
BF16 = jnp.bfloat16
LOG2E = 1.4426950408889634
NT = (((1,), (1,)), ((), ()))
TN = (((0,), (0,)), ((), ()))
SPAN = 512
LINE = 16
VMEM_GRANT = 63 * 1024 * 1024
TOK = 2 * SPAN
DIM = 128
SCALE = DIM ** -0.5


def tile(q, g, norm, delta, k, v, diagonal=False):
    score = lax.dot_general(k, q, NT, preferred_element_type=F32)
    prob = jnp.exp2(score * (SCALE * LOG2E) - norm)
    if diagonal:
        rows = lax.broadcasted_iota(jnp.int32, score.shape, 0)
        prob = jnp.where(rows <= lax.broadcasted_iota(jnp.int32, score.shape, 1), prob, 0.0)
    dprob = lax.dot_general(v, g, NT, preferred_element_type=F32)
    dscore = (prob * (dprob - delta)).astype(BF16)
    dv = jnp.dot(prob.astype(BF16), g, preferred_element_type=F32)
    dk = jnp.dot(dscore, q, preferred_element_type=F32)
    dq = lax.dot_general(dscore, k, TN, preferred_element_type=F32)
    return dq, dk, dv


def kernel(
    holders, heads, span_in, q_in, g_in, o_in, k_in, v_in, norm_in, dq_out, dk_out, dv_out,
    span_ref, raw_norm, raw_q, raw_g, raw_k, raw_v, raw_o, q_own, q_far, kv_own, kv_mate, kv_far,
    norm_own, norm_far, delta_own, delta_far, dq_acc, dk_acc, dv_acc, dq_end, dk_end, dv_end,
    mate_out, mate_part, next_out, dq_part, back_out, back_part, own_out, own_part,
    load_sem, kv_sem, mate_sem, far_sem, row_sem, dq_sem, back_send, back_recv, own_send, own_recv, hello, relay, plane,
):
    c = lax.axis_index("ctx")
    h = lax.axis_index("head")
    side = lax.rem(c, 2)
    even, odd = side == 0, side == 1
    mate = {"ctx": c + 1 - 2 * side}
    ahead = lax.rem(c + 2, holders)
    behind = lax.rem(c + holders - 2, holders)

    place_in_line = lax.rem(lax.div(c, 2), LINE)
    start_of_line, end_of_line = place_in_line == 0, place_in_line == LINE - 1
    is_odd_place = lax.rem(place_in_line, 2) == 1
    is_even_place = lax.rem(place_in_line, 2) == 0

    loads = [
        pltpu.make_async_copy(ref, raw, load_sem.at[i])
        for i, (ref, raw) in enumerate(
            (
                (span_in, span_ref), (k_in, raw_k), (v_in, raw_v), (q_in, raw_q), (g_in, raw_g),
                (norm_in, raw_norm), (o_in, raw_o),
            )
        )
    ]
    for copy in loads:
        copy.start()

    barrier = pltpu.get_barrier_semaphore()

    def tell(sem, **device):
        pl.semaphore_signal(sem, inc=1, device_id=device, device_id_type=MESH)

    def tell_heads(sem):
        for step in range(1, heads):
            tell(sem, head=lax.rem(h + step, heads))

    @pl.when(is_even_place)
    def _():
        for holder in (ahead, behind):
            tell(barrier, ctx=holder)
            tell(barrier, ctx=holder + 1 - 2 * side)
        tell_heads(barrier)

    wants_behind = jnp.logical_and(even, jnp.logical_not(start_of_line))

    @pl.when(jnp.logical_and(is_even_place, wants_behind))
    def _():
        pl.semaphore_wait(hello.at[1], 1)

    @pl.when(jnp.logical_and(is_even_place, jnp.logical_not(wants_behind)))
    def _():
        pl.semaphore_wait(hello.at[0], 1)

    @pl.when(is_odd_place)
    def _():
        tell(barrier, **mate)
        pl.semaphore_wait(barrier, 5)
        tell(hello.at[0], ctx=behind)
        tell(hello.at[1], ctx=ahead)

    loads[0].wait()

    def first(holder):
        return span_ref[2 * holder]

    def second(holder):
        return span_ref[2 * holder + 1]

    def low_span(holder):
        return jnp.minimum(first(holder), second(holder))

    def late(holder):
        return (first(holder) > second(holder)).astype(jnp.int32)

    low_place = late(c)
    asks = jnp.where(even, ahead, c)
    lows = [
        (low_span(c + 1 - 2 * side) < low_span(asks)).astype(jnp.int32),
        (low_span(jnp.where(even, c, behind)) < low_span(asks)).astype(jnp.int32),
    ]

    lo, hi = low_place * SPAN, (1 - low_place) * SPAN
    for copy in loads[1:5]:
        copy.wait()
    for i, (raw, place) in enumerate(((raw_q, hi), (raw_g, hi), (raw_q, lo), (raw_g, lo))):
        q_own[pl.ds(i * SPAN, SPAN)] = raw[pl.ds(place, SPAN)]
    for i, (raw, place) in enumerate(((raw_k, lo), (raw_v, lo), (raw_k, hi), (raw_v, hi))):
        kv_own[pl.ds(i * SPAN, SPAN)] = raw[pl.ds(place, SPAN)]
    def remote(src, dst, send, recv, device):
        return pltpu.make_async_remote_copy(
            src_ref=src, dst_ref=dst, send_sem=send, recv_sem=recv, device_id=device, device_id_type=MESH
        )

    half = lambda i: pl.ds(i * TOK, TOK)
    kv_copy = remote(kv_own, kv_mate, kv_sem.at[0], kv_sem.at[1], mate)
    q_copies = [
        remote(q_own.at[half(i)], q_far.at[half(i)], far_sem.at[0, i], far_sem.at[1, i], {"ctx": behind})
        for i in range(2)
    ]
    row_copies = [
        remote(own, far, row_sem.at[0, i], row_sem.at[1, i], {"ctx": behind})
        for i, (own, far) in enumerate(((norm_own, norm_far), (delta_own, delta_far)))
    ]
    back_copies = [
        remote(kv_own.at[half(i)], kv_far.at[half(i)], far_sem.at[0, i], far_sem.at[1, i], {"ctx": ahead})
        for i in range(2)
    ]

    @pl.when(odd)
    def _():
        back_copies[0].start()

    def send_queries():
        q_copies[0].start()

    pl.when(jnp.logical_and(even, jnp.logical_not(start_of_line)))(send_queries)
    kv_copy.start()

    for copy in loads[5:]:
        copy.wait()
    for i, place in enumerate((hi, lo)):
        norm_own[:, pl.ds(i * SPAN, SPAN)] = raw_norm[:, pl.ds(place, SPAN)] * LOG2E
        product = raw_g[pl.ds(place, SPAN)].astype(F32) * raw_o[pl.ds(place, SPAN)].astype(F32)
        delta_own[:, pl.ds(i * SPAN, SPAN)] = jnp.sum(product.T, axis=0, keepdims=True)

    def send_rows():
        for copy in row_copies:
            copy.start()

    pl.when(jnp.logical_and(even, jnp.logical_not(start_of_line)))(send_rows)

    def either(a, b):
        return a + b - 2 * a * b

    def at(i, size):
        return pl.ds(i * size, size)

    def block(qslot, qpart, kvslot, kvpart, diagonal=False):
        q, norm, delta = ((q_own, norm_own, delta_own), (q_far, norm_far, delta_far))[qslot]
        kv = (kv_own, kv_mate, kv_far)[kvslot]
        return tile(
            q[at(2 * qpart, SPAN)],
            q[at(2 * qpart + 1, SPAN)],
            norm[:, at(qpart, SPAN)],
            delta[:, at(qpart, SPAN)],
            kv[at(2 * kvpart, SPAN)],
            kv[at(2 * kvpart + 1, SPAN)],
            diagonal,
        )

    def crossing(qslot, kvslot, new_q, new_kv):
        dq, dk, dv = block(qslot, 0, kvslot, 0)
        top = pl.ds(0, SPAN)
        dq_acc[qslot, top] = dq if new_q else dq_acc[qslot, top] + dq
        dk_acc[kvslot, top] = dk if new_kv else dk_acc[kvslot, top] + dk
        dv_acc[kvslot, top] = dv if new_kv else dv_acc[kvslot, top] + dv

    def level(pair, qslot, kvslot):
        dq, dk, dv = block(qslot, lows[pair], kvslot, 1 - lows[pair])
        top = pl.ds(0, SPAN)
        dq_end[pair, top] = dq
        dk_end[pair, top] = dk
        dv_end[pair, top] = dv

    crossing(0, 0, True, True)
    dq, dk, dv = block(0, 1, 0, 0, True)
    dq_acc[0, pl.ds(SPAN, SPAN)] = dq
    dk_acc[0, pl.ds(0, SPAN)] += dk
    dv_acc[0, pl.ds(0, SPAN)] += dv
    dq, dk, dv = block(0, 0, 0, 1, True)
    dq_acc[0, pl.ds(0, SPAN)] += dq
    dk_acc[0, pl.ds(SPAN, SPAN)] = dk
    dv_acc[0, pl.ds(SPAN, SPAN)] = dv

    @pl.when(odd)
    def _():
        back_copies[1].start()

    pl.when(jnp.logical_and(even, jnp.logical_not(start_of_line)))(q_copies[1].start)

    @pl.when(jnp.logical_and(is_even_place, wants_behind))
    def _():
        pl.semaphore_wait(hello.at[0], 1)

    @pl.when(is_even_place)
    def _():
        pl.semaphore_wait(barrier, heads - 1)
        tell_heads(relay)

    @pl.when(jnp.logical_and(even, start_of_line))
    def _():
        pl.semaphore_wait(hello.at[1], 1)

    pl.when(jnp.logical_and(even, start_of_line))(send_queries)
    pl.when(jnp.logical_and(even, start_of_line))(send_rows)

    def tell_ahead():
        @pl.when(is_even_place)
        def _():
            pl.semaphore_wait(relay, heads - 1)
            tell(plane, ctx=ahead)

    for ref in (dq_end, dk_end, dv_end):
        for pair in range(2):
            ref[pair, pl.ds(SPAN, SPAN)] = jnp.zeros((SPAN, DIM), F32)

    def if_low(pair, part, end, on=1):
        return end[pair, at(1 - on * either(lows[pair], part), SPAN)]

    mate_copy = remote(mate_out, mate_part, mate_sem.at[0], mate_sem.at[1], mate)

    def send_mate():
        for part in range(2):
            for i, (acc, end, factor) in enumerate(((dk_acc, dk_end, SCALE), (dv_acc, dv_end, 1.0))):
                value = if_low(0, part, end)
                if part == 0:
                    value += acc[1, pl.ds(0, SPAN)]
                mate_out[pl.ds(part * TOK + i * SPAN, SPAN)] = (value * factor).astype(BF16)
        mate_copy.start()

    dq_copy = remote(next_out, dq_part, dq_sem.at[0], dq_sem.at[1], {"ctx": ahead})
    chunks = heads // 2
    each = TOK // heads
    order = [lax.rem(h + step, chunks) for step in range(1, chunks + 1)]

    def chunk_copy(i):
        return remote(back_out.at[i], back_part.at[i], back_send.at[i], back_recv.at[i], {"ctx": behind})

    def send_back(block, dk, dv):
        for r in range(chunks):
            rows = slice(r * each, (r + 1) * each)
            back_out[block * chunks + r, pl.ds(0, each)] = (dk[rows] * SCALE).astype(BF16)
            back_out[block * chunks + r, pl.ds(each, each)] = dv[rows].astype(BF16)
        for r in order:
            chunk_copy(block * chunks + r).start()

    @pl.when(even)
    def _():
        kv_copy.wait_recv()
        for copy in row_copies:
            copy.wait_recv()
        tell_ahead()
        q_copies[0].wait_recv()
        crossing(1, 1, True, True)
        crossing(1, 0, False, False)
        pl.when(start_of_line)(q_copies[1].start)
        q_copies[1].wait_recv()
        level(0, 1, 1)
        pl.when(jnp.logical_not(end_of_line))(send_mate)
        level(1, 1, 0)
        for part in range(2):
            value = if_low(0, 1 - part, dq_end) + if_low(1, 1 - part, dq_end)
            if part == 0:
                value += dq_acc[1, pl.ds(0, SPAN)]
            next_out[pl.ds(part * SPAN, SPAN)] = (value * SCALE).astype(BF16)
        dq_copy.start()
        pl.when(end_of_line)(send_mate)

    low_of = [low_place, 1 - low_place]

    def visit_behind():
        @pl.when(is_even_place)
        def _():
            pl.semaphore_wait(hello.at[1], 1)

        back_copies[0].wait_recv()
        dq, dk, dv = block(0, 0, 2, 0)
        dq_acc[0, pl.ds(0, SPAN)] += dq
        send_back(0, dk, dv)
        back_copies[1].wait_recv()
        dq, dk, dv = block(0, lows[1], 2, 1 - lows[1])
        dq_end[1, pl.ds(0, SPAN)] = dq
        send_back(1, dk, dv)

    @pl.when(odd)
    def _():
        kv_copy.wait_recv()
        crossing(0, 1, False, True)
        level(0, 0, 1)
        send_mate()
        tell_ahead()

    pl.when(odd)(visit_behind)

    mate_copy.wait_recv()

    @pl.when(is_odd_place)
    def _():
        pl.semaphore_wait(plane, 1)

    def own_copy(to):
        return remote(own_out.at[to], own_part.at[h], own_send.at[to], own_recv.at[h], {"head": to})

    next_low = (low_span(c) < low_span(ahead)).astype(jnp.int32)
    for step, r in enumerate(order):

        @pl.when(odd)
        def _():
            chunk_copy(r).wait_recv()
            chunk_copy(chunks + r).wait_recv()

        for p in range(2):
            part = low_of[p]
            to = p * chunks + r
            row = r * each

            def rows_of(i):
                return pl.ds(i * SPAN + row, each)

            halves = []
            for i, (acc, end, factor) in enumerate(((dk_acc, dk_end, SCALE), (dv_acc, dv_end, 1.0))):
                add = end[1, rows_of(1 - (1 - side) * either(lows[1], part))]
                value = (acc[0, rows_of(part)] + add) * factor
                halves.append(value + mate_part[rows_of(2 * part + i)].astype(F32))

            @pl.when(even)
            def _():
                for i in range(2):
                    own_out[to, pl.ds(i * each, each)] = halves[i].astype(BF16)

            @pl.when(odd)
            def _():
                for i in range(2):
                    value = halves[i]
                    for place, on in ((r, 1 - part), (chunks + r, either(next_low, part))):
                        there = jnp.full((each, DIM), on, jnp.int32) == 1
                        back = back_part[place, pl.ds(i * each, each)].astype(F32)
                        value += jnp.where(there, back, 0.0)
                    own_out[to, pl.ds(i * each, each)] = value.astype(BF16)

            if step < chunks - 1:
                own_copy(to).start()
            else:
                pl.when(to != h)(own_copy(to).start)
    own_part[h] = own_out[h]

    def finish_queries():
        dq_copy.wait_recv()
        for p in range(2):
            place = (1 - low_of[p]) * SPAN
            value = dq_acc[0, pl.ds(place, SPAN)] * SCALE + dq_part[pl.ds(place, SPAN)].astype(F32)
            dq_out[pl.ds(p * SPAN, SPAN)] = value.astype(BF16)

    pl.when(wants_behind)(finish_queries)

    @pl.when(odd)
    def _():
        for p in range(2):
            place = (1 - low_of[p]) * SPAN
            value = dq_acc[0, pl.ds(place, SPAN)]
            value += if_low(0, low_of[p], dq_end) + if_low(1, low_of[p], dq_end)
            dq_out[pl.ds(p * SPAN, SPAN)] = (value * SCALE).astype(BF16)

    for step in range(1, heads):
        sender = lax.rem(h + step, heads)
        remote(own_out.at[sender], own_part.at[sender], own_send.at[sender], own_recv.at[sender], mate).wait_recv()
    total = own_part[0].astype(F32)
    for i in range(1, heads):
        total += own_part[i].astype(F32)
    dk_out[...] = total[:each].astype(BF16)
    dv_out[...] = total[each:].astype(BF16)
    pl.when(jnp.logical_and(even, start_of_line))(finish_queries)

    kv_copy.wait_send()
    mate_copy.wait_send()
    for step in range(1, heads):
        own_copy(lax.rem(h + step, heads)).wait_send()

    @pl.when(even)
    def _():
        for copy in (*row_copies, *q_copies, dq_copy):
            copy.wait_send()

    @pl.when(odd)
    def _():
        for copy in (*back_copies, *(chunk_copy(i) for i in range(heads))):
            copy.wait_send()


def store(dq, dk, dv, dq_out, dk_out, dv_out, sem):
    copies = [
        pltpu.make_async_copy(src, dst, sem.at[i])
        for i, (src, dst) in enumerate(((dq, dq_out), (dk, dk_out), (dv, dv_out)))
    ]
    for copy in copies:
        copy.start()
    for copy in copies:
        copy.wait()


def local(queries, keys, values, outputs, out_grad, log_norm, span_ids):
    holders, heads = lax.axis_size("ctx"), lax.axis_size("head")
    each = TOK // heads
    flat = lambda a: a.reshape(TOK, DIM)
    body = lambda *refs: kernel(holders, heads, *refs)
    dma = pltpu.SemaphoreType.DMA
    dq, dk, dv = pl.pallas_call(
        body,
        out_shape=[
            jax.ShapeDtypeStruct((TOK, DIM), BF16),
            jax.ShapeDtypeStruct((each, DIM), BF16),
            jax.ShapeDtypeStruct((each, DIM), BF16),
        ],
        in_specs=[
            *[pl.BlockSpec(memory_space=pltpu.HBM)] * 7,
        ],
        out_specs=[pl.BlockSpec(memory_space=pltpu.VMEM)] * 3,
        scratch_shapes=[
            pltpu.SMEM((2 * holders,), jnp.int32),
            pltpu.VMEM((1, TOK), F32),
            *[pltpu.VMEM((TOK, DIM), BF16)] * 5,
            *[pltpu.VMEM((2 * TOK, DIM), BF16)] * 5,
            *[pltpu.VMEM((1, TOK), F32)] * 4,
            pltpu.VMEM((2, TOK, DIM), F32),
            pltpu.VMEM((2, TOK, DIM), F32),
            pltpu.VMEM((2, TOK, DIM), F32),
            pltpu.VMEM((2, TOK, DIM), F32),
            pltpu.VMEM((2, TOK, DIM), F32),
            pltpu.VMEM((2, TOK, DIM), F32),
            pltpu.VMEM((2 * TOK, DIM), BF16),
            pltpu.VMEM((2 * TOK, DIM), BF16),
            pltpu.VMEM((TOK, DIM), BF16),
            pltpu.VMEM((TOK, DIM), BF16),
            pltpu.VMEM((heads, 2 * each, DIM), BF16),
            pltpu.VMEM((heads, 2 * each, DIM), BF16),
            pltpu.VMEM((heads, 2 * each, DIM), BF16),
            pltpu.VMEM((heads, 2 * each, DIM), BF16),
            dma((7,)),
            dma((2,)),
            dma((2,)),
            dma((2, 2)),
            dma((2, 2)),
            dma((2,)),
            dma((heads,)),
            dma((heads,)),
            dma((heads,)),
            dma((heads,)),
            pltpu.SemaphoreType.REGULAR((2,)),
            pltpu.SemaphoreType.REGULAR,
            pltpu.SemaphoreType.REGULAR,
        ],
        compiler_params=pltpu.CompilerParams(
            collective_id=0, has_side_effects=True, vmem_limit_bytes=VMEM_GRANT
        ),
    )(
        span_ids,
        flat(queries),
        flat(out_grad),
        flat(outputs),
        keys,
        values,
        log_norm,
    )
    dq, dk, dv = pl.pallas_call(
        store,
        out_shape=[jax.ShapeDtypeStruct(a.shape, BF16) for a in (dq, dk, dv)],
        in_specs=[pl.BlockSpec(memory_space=pltpu.VMEM)] * 3,
        out_specs=[pl.BlockSpec(memory_space=pltpu.HBM)] * 3,
        scratch_shapes=[dma((3,))],
    )(dq, dk, dv)
    return dq.reshape(queries.shape), dk, dv


def solution(mesh):
    in_specs = (
        P("ctx", "head", None),
        P("ctx", None),
        P("ctx", None),
        P("ctx", "head", None),
        P("ctx", "head", None),
        P("head", "ctx"),
        P(),
    )
    out_specs = (P("ctx", "head", None), P(("ctx", "head"), None), P(("ctx", "head"), None))
    return jax.shard_map(local, mesh=mesh, in_specs=in_specs, out_specs=out_specs, check_vma=False)
```

```python
import jax
import jax.numpy as jnp
from jax import lax
from jax.experimental import pallas as pl
from jax.experimental.pallas import tpu as pltpu
from jax.sharding import PartitionSpec as P

MESH = pl.DeviceIdType.MESH
F32 = jnp.float32
BF16 = jnp.bfloat16
LOG2E = 1.4426950408889634
NT = (((1,), (1,)), ((), ()))
TN = (((0,), (0,)), ((), ()))
SPAN = 512
LINE = 16
VMEM_GRANT = 63 * 1024 * 1024
TOK = 2 * SPAN
DIM = 128
SCALE = DIM ** -0.5


def tile(q, g, norm, delta, k, v, diagonal=False):
    score = lax.dot_general(k, q, NT, preferred_element_type=F32)
    prob = jnp.exp2(score * (SCALE * LOG2E) - norm)
    if diagonal:
        rows = lax.broadcasted_iota(jnp.int32, score.shape, 0)
        prob = jnp.where(rows <= lax.broadcasted_iota(jnp.int32, score.shape, 1), prob, 0.0)
    dprob = lax.dot_general(v, g, NT, preferred_element_type=F32)
    dscore = (prob * (dprob - delta)).astype(BF16)
    dv = jnp.dot(prob.astype(BF16), g, preferred_element_type=F32)
    dk = jnp.dot(dscore, q, preferred_element_type=F32)
    dq = lax.dot_general(dscore, k, TN, preferred_element_type=F32)
    return dq, dk, dv


def kernel(
    holders, heads, span_in, q_in, g_in, o_in, k_in, v_in, norm_in, dq_out, dkv_out,
    span_ref, raw_norm, raw_q, raw_g, raw_k, raw_v, raw_o, q_own, kv_own, kv_mate,
    *rest,
):
    chunks = heads // 2
    q_far, kv_far, dq_part, back_part = (rest[i * chunks : (i + 1) * chunks] for i in range(4))
    (
        norm_own, norm_far, delta_own, delta_far, dq_acc, dk_acc, dv_acc, dq_end, dk_end, dv_end,
        mate_out, mate_part, next_out, back_out, own_out, own_part,
        load_sem, kv_sem, mate_sem, far_sem, row_sem, dq_sem, back_sem, own_send, own_recv,
        hello, relay, plane,
    ) = rest[4 * chunks :]
    each = TOK // heads
    c = lax.axis_index("ctx")
    h = lax.axis_index("head")
    side = lax.rem(c, 2)
    even, odd = side == 0, side == 1
    mate = {"ctx": c + 1 - 2 * side}
    ahead = lax.rem(c + 2, holders)
    behind = lax.rem(c + holders - 2, holders)

    place_in_line = lax.rem(lax.div(c, 2), LINE)
    start_of_line, end_of_line = place_in_line == 0, place_in_line == LINE - 1
    is_odd_place = lax.rem(place_in_line, 2) == 1
    is_even_place = lax.rem(place_in_line, 2) == 0

    loads = [
        pltpu.make_async_copy(ref, raw, load_sem.at[i])
        for i, (ref, raw) in enumerate(
            (
                (span_in, span_ref), (k_in, raw_k), (v_in, raw_v), (q_in, raw_q), (g_in, raw_g),
                (norm_in, raw_norm), (o_in, raw_o),
            )
        )
    ]
    for copy in loads:
        copy.start()

    barrier = pltpu.get_barrier_semaphore()

    def tell(sem, **device):
        pl.semaphore_signal(sem, inc=1, device_id=device, device_id_type=MESH)

    def tell_heads(sem):
        for step in range(1, heads):
            tell(sem, head=lax.rem(h + step, heads))

    @pl.when(is_even_place)
    def _():
        for holder in (ahead, behind):
            tell(barrier, ctx=holder)
            tell(barrier, ctx=holder + 1 - 2 * side)
        tell_heads(barrier)

    wants_behind = jnp.logical_and(even, jnp.logical_not(start_of_line))

    @pl.when(jnp.logical_and(is_even_place, wants_behind))
    def _():
        pl.semaphore_wait(hello.at[1], 1)

    @pl.when(jnp.logical_and(is_even_place, jnp.logical_not(wants_behind)))
    def _():
        pl.semaphore_wait(hello.at[0], 1)

    @pl.when(is_odd_place)
    def _():
        tell(barrier, **mate)
        pl.semaphore_wait(barrier, 5)
        tell(hello.at[0], ctx=behind)
        tell(hello.at[1], ctx=ahead)

    loads[0].wait()

    def first(holder):
        return span_ref[2 * holder]

    def second(holder):
        return span_ref[2 * holder + 1]

    def low_span(holder):
        return jnp.minimum(first(holder), second(holder))

    def late(holder):
        return (first(holder) > second(holder)).astype(jnp.int32)

    low_place = late(c)
    asks = jnp.where(even, ahead, c)
    lows = [
        (low_span(c + 1 - 2 * side) < low_span(asks)).astype(jnp.int32),
        (low_span(jnp.where(even, c, behind)) < low_span(asks)).astype(jnp.int32),
    ]

    lo, hi = low_place * SPAN, (1 - low_place) * SPAN

    def by_chunk(ref, i, value):
        for r in range(chunks):
            ref[r, pl.ds(i * each, each)] = value[r * each : (r + 1) * each]

    for copy in loads[1:5]:
        copy.wait()
    for i, (raw, place) in enumerate(((raw_q, hi), (raw_g, hi), (raw_q, lo), (raw_g, lo))):
        by_chunk(q_own, i, raw[pl.ds(place, SPAN)])
    for i, (raw, place) in enumerate(((raw_k, lo), (raw_v, lo), (raw_k, hi), (raw_v, hi))):
        by_chunk(kv_own, i, raw[pl.ds(place, SPAN)])

    def remote(src, dst, send, recv, device):
        return pltpu.make_async_remote_copy(
            src_ref=src, dst_ref=dst, send_sem=send, recv_sem=recv, device_id=device, device_id_type=MESH
        )

    order = [lax.rem(h + step, chunks) for step in range(1, chunks + 1)]
    kv_copy = remote(kv_own, kv_mate, kv_sem.at[0], kv_sem.at[1], mate)
    q_copies = [
        remote(q_own.at[j], q_far[j], far_sem.at[0, j], far_sem.at[1, j], {"ctx": behind}) for j in range(chunks)
    ]
    kv_copies = [
        remote(kv_own.at[order[j]], kv_far[j], far_sem.at[0, j], far_sem.at[1, j], {"ctx": ahead})
        for j in range(chunks)
    ]
    row_copies = [
        remote(own, far, row_sem.at[0, i], row_sem.at[1, i], {"ctx": behind})
        for i, (own, far) in enumerate(((norm_own, norm_far), (delta_own, delta_far)))
    ]
    dq_copies = [
        remote(next_out.at[j], dq_part[j], dq_sem.at[0, j], dq_sem.at[1, j], {"ctx": ahead}) for j in range(chunks)
    ]
    back_copies = [
        remote(back_out.at[j], back_part[j], back_sem.at[0, j], back_sem.at[1, j], {"ctx": behind})
        for j in range(chunks)
    ]
    mate_copy = remote(mate_out, mate_part, mate_sem.at[0], mate_sem.at[1], mate)
    starts_line = jnp.logical_and(even, start_of_line)

    def send_chunk(j):
        pl.when(odd)(kv_copies[j].start)
        pl.when(wants_behind)(q_copies[j].start)

    send_chunk(0)
    kv_copy.start()

    for copy in loads[5:]:
        copy.wait()
    for i, place in enumerate((hi, lo)):
        norm_own[:, pl.ds(i * SPAN, SPAN)] = raw_norm[:, pl.ds(place, SPAN)] * LOG2E
        product = raw_g[pl.ds(place, SPAN)].astype(F32) * raw_o[pl.ds(place, SPAN)].astype(F32)
        delta_own[:, pl.ds(i * SPAN, SPAN)] = jnp.sum(product.T, axis=0, keepdims=True)

    def send_rows():
        for copy in row_copies:
            copy.start()

    pl.when(wants_behind)(send_rows)

    def either(a, b):
        return a + b - 2 * a * b

    def at(i, size):
        return pl.ds(i * size, size)

    def whole(ref, i):
        return ref[:, at(i, each)].reshape(SPAN, DIM)

    def block(qpart, kv, kvpart, diagonal=False):
        return tile(
            whole(q_own, 2 * qpart),
            whole(q_own, 2 * qpart + 1),
            norm_own[:, at(qpart, SPAN)],
            delta_own[:, at(qpart, SPAN)],
            whole(kv, 2 * kvpart),
            whole(kv, 2 * kvpart + 1),
            diagonal,
        )

    top, bottom = pl.ds(0, SPAN), pl.ds(SPAN, SPAN)

    dq, dk, dv = block(0, kv_own, 0)
    dq_acc[top] = dq
    dk_acc[0, top] = dk
    dv_acc[0, top] = dv
    send_chunk(1)
    dq, dk, dv = block(1, kv_own, 0, True)
    dq_acc[bottom] = dq
    dk_acc[0, top] += dk
    dv_acc[0, top] += dv
    send_chunk(2)
    dq, dk, dv = block(0, kv_own, 1, True)
    dq_acc[top] += dq
    dk_acc[0, bottom] = dk
    dv_acc[0, bottom] = dv
    send_chunk(3)

    @pl.when(jnp.logical_and(is_even_place, wants_behind))
    def _():
        pl.semaphore_wait(hello.at[0], 1)

    @pl.when(is_even_place)
    def _():
        pl.semaphore_wait(barrier, heads - 1)
        tell_heads(relay)

    @pl.when(starts_line)
    def _():
        pl.semaphore_wait(hello.at[1], 1)
        q_copies[0].start()
        send_rows()

    def tell_ahead():
        @pl.when(is_even_place)
        def _():
            pl.semaphore_wait(relay, heads - 1)
            tell(plane, ctx=ahead)

    for ref in (dq_end, dk_end, dv_end):
        for pair in range(2):
            ref[pair, bottom] = jnp.zeros((SPAN, DIM), F32)

    def if_low(pair, part, end, on=1):
        return end[pair, at(1 - on * either(lows[pair], part), SPAN)]

    def split(pair, value):
        is_low = jnp.full(value.shape, lows[pair], jnp.int32) == 1
        return jnp.where(is_low, value, 0.0), jnp.where(is_low, 0.0, value)

    def send_mate():
        for part in range(2):
            for i, (acc, end, factor) in enumerate(((dk_acc, dk_end, SCALE), (dv_acc, dv_end, 1.0))):
                value = if_low(0, part, end)
                if part == 0:
                    value += acc[1, top]
                mate_out[pl.ds(part * TOK + i * SPAN, SPAN)] = (value * factor).astype(BF16)
        mate_copy.start()

    def add(ref, index, value, first):
        ref[index] = value if first else ref[index] + value

    @pl.when(even)
    def _():
        kv_copy.wait_recv()
        for copy in row_copies:
            copy.wait_recv()
        tell_ahead()
        for j in range(chunks):
            if j + 1 < chunks:
                pl.when(starts_line)(q_copies[j + 1].start)
            q_copies[j].wait_recv()
            q = q_far[j]
            dq_hi = dq_lo = 0.0
            for pair, kv, slot in ((0, kv_mate, 1), (1, kv_own, 0)):
                row = pl.ds(j * each, each)
                dq, dk, dv = tile(
                    q[at(0, each)], q[at(1, each)], norm_far[:, row], delta_far[:, row], whole(kv, 0), whole(kv, 1)
                )
                dq_hi += dq
                add(dk_acc, (slot, top), dk, j == 0 and slot == 1)
                add(dv_acc, (slot, top), dv, j == 0 and slot == 1)
                is_low = lows[pair]
                row = pl.ds(is_low * SPAN + j * each, each)
                dq, dk, dv = tile(
                    q[at(2 * is_low, each)],
                    q[at(2 * is_low + 1, each)],
                    norm_far[:, row],
                    delta_far[:, row],
                    whole(kv, 2 * (1 - is_low)),
                    whole(kv, 2 * (1 - is_low) + 1),
                )
                to_lo, to_hi = split(pair, dq)
                dq_lo += to_lo
                dq_hi += to_hi
                add(dk_end, (pair, top), dk, j == 0)
                add(dv_end, (pair, top), dv, j == 0)
            next_out[j, at(0, each)] = (dq_hi * SCALE).astype(BF16)
            next_out[j, at(1, each)] = (dq_lo * SCALE).astype(BF16)
            dq_copies[j].start()
        send_mate()

    @pl.when(odd)
    def _():
        kv_copy.wait_recv()
        dq, dk, dv = block(0, kv_mate, 0)
        dq_acc[top] += dq
        dk_acc[1, top] = dk
        dv_acc[1, top] = dv
        dq, dk, dv = block(lows[0], kv_mate, 1 - lows[0])
        dq_end[0, top] = dq
        dk_end[0, top] = dk
        dv_end[0, top] = dv
        send_mate()
        tell_ahead()

    low_of = [low_place, 1 - low_place]

    def visit_behind():
        @pl.when(is_even_place)
        def _():
            pl.semaphore_wait(hello.at[1], 1)

        is_low = lows[1]
        for j in range(chunks):
            kv_copies[j].wait_recv()
            kv = kv_far[j]
            dq, dk, dv = tile(
                whole(q_own, 0), whole(q_own, 1), norm_own[:, top], delta_own[:, top], kv[at(0, each)], kv[at(1, each)]
            )
            dq_acc[top] += dq
            dq, dk_end_j, dv_end_j = tile(
                whole(q_own, 2 * is_low),
                whole(q_own, 2 * is_low + 1),
                norm_own[:, at(is_low, SPAN)],
                delta_own[:, at(is_low, SPAN)],
                kv[at(2 * (1 - is_low), each)],
                kv[at(2 * (1 - is_low) + 1, each)],
            )
            add(dq_end, (1, top), dq, j == 0)
            for i, (value, end, factor) in enumerate(((dk, dk_end_j, SCALE), (dv, dv_end_j, 1.0))):
                to_lo, to_hi = split(1, end)
                back_out[j, at(i, each)] = ((value + to_lo) * factor).astype(BF16)
                back_out[j, at(2 + i, each)] = (to_hi * factor).astype(BF16)
            back_copies[j].start()
        for p in range(2):
            value = dq_acc[at(1 - low_of[p], SPAN)]
            value += if_low(0, low_of[p], dq_end) + if_low(1, low_of[p], dq_end)
            dq_out[pl.ds(p * SPAN, SPAN)] = (value * SCALE).astype(BF16)

    pl.when(jnp.logical_and(odd, jnp.logical_not(start_of_line)))(visit_behind)

    mate_copy.wait_recv()

    @pl.when(is_odd_place)
    def _():
        pl.semaphore_wait(plane, 1)

    def own_copy(to):
        return remote(own_out.at[to], own_part.at[h], own_send.at[to], own_recv.at[h], {"head": to})

    for j, r in enumerate(order):
        pl.when(odd)(back_copies[j].wait_recv)
        for p in range(2):
            part = low_of[p]
            to = p * chunks + r
            row = r * each

            def rows_of(i):
                return pl.ds(i * SPAN + row, each)

            halves = []
            for i, (acc, end, factor) in enumerate(((dk_acc, dk_end, SCALE), (dv_acc, dv_end, 1.0))):
                more = end[1, rows_of(1 - (1 - side) * either(lows[1], part))]
                value = (acc[0, rows_of(part)] + more) * factor
                halves.append(value + mate_part[rows_of(2 * part + i)].astype(F32))

            @pl.when(even)
            def _():
                for i in range(2):
                    own_out[to, at(i, each)] = halves[i].astype(BF16)

            @pl.when(odd)
            def _():
                for i in range(2):
                    back = back_part[j][at(2 * part + i, each)].astype(F32)
                    own_out[to, at(i, each)] = (halves[i] + back).astype(BF16)

            if j < chunks - 1:
                own_copy(to).start()
            else:
                pl.when(to != h)(own_copy(to).start)
    own_part[h] = own_out[h]

    pl.when(jnp.logical_and(odd, start_of_line))(visit_behind)

    def finish_queries():
        for j in range(chunks):
            dq_copies[j].wait_recv()
            for p in range(2):
                place = 1 - low_of[p]
                own = dq_acc[pl.ds(place * SPAN + j * each, each)] * SCALE
                far = dq_part[j][at(place, each)].astype(F32)
                dq_out[pl.ds(p * SPAN + j * each, each)] = (own + far).astype(BF16)

    pl.when(wants_behind)(finish_queries)

    for step in range(1, heads):
        sender = lax.rem(h + step, heads)
        remote(own_out.at[sender], own_part.at[sender], own_send.at[sender], own_recv.at[sender], mate).wait_recv()
    total = own_part[0].astype(F32)
    for i in range(1, heads):
        total += own_part[i].astype(F32)
    dkv_out[...] = total.astype(BF16)
    pl.when(starts_line)(finish_queries)

    kv_copy.wait_send()
    mate_copy.wait_send()
    for step in range(1, heads):
        own_copy(lax.rem(h + step, heads)).wait_send()

    @pl.when(even)
    def _():
        for copy in (*row_copies, *q_copies, *dq_copies):
            copy.wait_send()

    @pl.when(odd)
    def _():
        for copy in (*kv_copies, *back_copies):
            copy.wait_send()


def local(queries, keys, values, outputs, out_grad, log_norm, span_ids):
    holders, heads = lax.axis_size("ctx"), lax.axis_size("head")
    each, chunks = TOK // heads, heads // 2
    flat = lambda a: a.reshape(TOK, DIM)
    body = lambda *refs: kernel(holders, heads, *refs)
    dma = pltpu.SemaphoreType.DMA
    dq, dkv = pl.pallas_call(
        body,
        out_shape=[
            pltpu.VMEM((TOK, DIM), BF16),
            pltpu.VMEM((2 * each, DIM), BF16),
        ],
        in_specs=[
            *[pl.BlockSpec(memory_space=pltpu.HBM)] * 7,
        ],
        out_specs=[pl.BlockSpec(memory_space=pltpu.VMEM)] * 2,
        scratch_shapes=[
            pltpu.SMEM((2 * holders,), jnp.int32),
            pltpu.VMEM((1, TOK), F32),
            *[pltpu.VMEM((TOK, DIM), BF16)] * 5,
            *[pltpu.VMEM((chunks, 4 * each, DIM), BF16)] * 3,
            *[pltpu.VMEM((4 * each, DIM), BF16)] * (2 * chunks),
            *[pltpu.VMEM((2 * each, DIM), BF16)] * chunks,
            *[pltpu.VMEM((4 * each, DIM), BF16)] * chunks,
            *[pltpu.VMEM((1, TOK), F32)] * 4,
            pltpu.VMEM((TOK, DIM), F32),
            *[pltpu.VMEM((2, TOK, DIM), F32)] * 5,
            pltpu.VMEM((2 * TOK, DIM), BF16),
            pltpu.VMEM((2 * TOK, DIM), BF16),
            pltpu.VMEM((chunks, 2 * each, DIM), BF16),
            pltpu.VMEM((chunks, 4 * each, DIM), BF16),
            pltpu.VMEM((heads, 2 * each, DIM), BF16),
            pltpu.VMEM((heads, 2 * each, DIM), BF16),
            dma((7,)),
            dma((2,)),
            dma((2,)),
            dma((2, chunks)),
            dma((2, 2)),
            dma((2, chunks)),
            dma((2, chunks)),
            dma((heads,)),
            dma((heads,)),
            pltpu.SemaphoreType.REGULAR((2,)),
            pltpu.SemaphoreType.REGULAR,
            pltpu.SemaphoreType.REGULAR,
        ],
        compiler_params=pltpu.CompilerParams(
            collective_id=0, has_side_effects=True, vmem_limit_bytes=VMEM_GRANT
        ),
    )(
        span_ids,
        flat(queries),
        flat(out_grad),
        flat(outputs),
        keys,
        values,
        log_norm,
    )
    return dq.reshape(queries.shape), dkv[:each], dkv[each:]


def solution(mesh):
    in_specs = (
        P("ctx", "head", None),
        P("ctx", None),
        P("ctx", None),
        P("ctx", "head", None),
        P("ctx", "head", None),
        P("head", "ctx"),
        P(),
    )
    out_specs = (P("ctx", "head", None), P(("ctx", "head"), None), P(("ctx", "head"), None))
    return jax.shard_map(local, mesh=mesh, in_specs=in_specs, out_specs=out_specs, check_vma=False)
```

```python
import jax
import jax.numpy as jnp
from jax import lax
from jax.experimental import pallas as pl
from jax.experimental.pallas import tpu as pltpu
from jax.sharding import PartitionSpec as P

MESH = pl.DeviceIdType.MESH
F32 = jnp.float32
BF16 = jnp.bfloat16
LOG2E = 1.4426950408889634
NT = (((1,), (1,)), ((), ()))
TN = (((0,), (0,)), ((), ()))
SPAN = 512
LINE = 16
VMEM_GRANT = 63 * 1024 * 1024
TOK = 2 * SPAN
DIM = 128
SCALE = DIM ** -0.5


def tile(q, g, norm, delta, k, v, diagonal=False):
    score = lax.dot_general(k, q, NT, preferred_element_type=F32)
    prob = jnp.exp2(score * (SCALE * LOG2E) - norm)
    if diagonal:
        rows = lax.broadcasted_iota(jnp.int32, score.shape, 0)
        prob = jnp.where(rows <= lax.broadcasted_iota(jnp.int32, score.shape, 1), prob, 0.0)
    dprob = lax.dot_general(v, g, NT, preferred_element_type=F32)
    dscore = (prob * (dprob - delta)).astype(BF16)
    dv = jnp.dot(prob.astype(BF16), g, preferred_element_type=F32)
    dk = jnp.dot(dscore, q, preferred_element_type=F32)
    dq = lax.dot_general(dscore, k, TN, preferred_element_type=F32)
    return dq, dk, dv


def kernel(
    holders, heads, span_in, q_in, g_in, o_in, k_in, v_in, norm_in, dq_out, dkv_out,
    span_ref, raw_norm, raw_q, raw_g, raw_k, raw_v, raw_o, q_own, kv_own, kv_mate,
    *rest,
):
    chunks = heads // 2
    q_far, kv_far, dq_part, back_part = (rest[i * chunks : (i + 1) * chunks] for i in range(4))
    (
        norm_own, norm_far, delta_own, delta_far, dq_acc, dk_acc, dv_acc, dq_end, dk_end, dv_end,
        mate_out, mate_part, next_out, back_out, own_out, own_part,
        load_sem, kv_sem, mate_sem, far_sem, row_sem, dq_sem, back_sem, own_send, own_recv,
        hello, relay, plane,
    ) = rest[4 * chunks :]
    each = TOK // heads
    c = lax.axis_index("ctx")
    h = lax.axis_index("head")
    side = lax.rem(c, 2)
    even, odd = side == 0, side == 1
    mate = {"ctx": c + 1 - 2 * side}
    ahead = lax.rem(c + 2, holders)
    behind = lax.rem(c + holders - 2, holders)

    place_in_line = lax.rem(lax.div(c, 2), LINE)
    start_of_line, end_of_line = place_in_line == 0, place_in_line == LINE - 1
    is_odd_place = lax.rem(place_in_line, 2) == 1
    is_even_place = lax.rem(place_in_line, 2) == 0

    loads = [
        pltpu.make_async_copy(ref, raw, load_sem.at[i])
        for i, (ref, raw) in enumerate(
            (
                (span_in, span_ref), (k_in, raw_k), (v_in, raw_v), (q_in, raw_q), (g_in, raw_g),
                (norm_in, raw_norm), (o_in, raw_o),
            )
        )
    ]
    for copy in loads:
        copy.start()

    barrier = pltpu.get_barrier_semaphore()

    def tell(sem, **device):
        pl.semaphore_signal(sem, inc=1, device_id=device, device_id_type=MESH)

    def tell_heads(sem):
        for step in range(1, heads):
            tell(sem, head=lax.rem(h + step, heads))

    @pl.when(is_even_place)
    def _():
        for holder in (ahead, behind):
            tell(barrier, ctx=holder)
            tell(barrier, ctx=holder + 1 - 2 * side)
        tell_heads(barrier)

    wants_behind = jnp.logical_and(even, jnp.logical_not(start_of_line))

    @pl.when(jnp.logical_and(is_even_place, wants_behind))
    def _():
        pl.semaphore_wait(hello.at[1], 1)

    @pl.when(jnp.logical_and(is_even_place, jnp.logical_not(wants_behind)))
    def _():
        pl.semaphore_wait(hello.at[0], 1)

    @pl.when(is_odd_place)
    def _():
        tell(barrier, **mate)
        pl.semaphore_wait(barrier, 5)
        tell(hello.at[0], ctx=behind)
        tell(hello.at[1], ctx=ahead)

    loads[0].wait()

    def first(holder):
        return span_ref[2 * holder]

    def second(holder):
        return span_ref[2 * holder + 1]

    def low_span(holder):
        return jnp.minimum(first(holder), second(holder))

    def late(holder):
        return (first(holder) > second(holder)).astype(jnp.int32)

    low_place = late(c)
    asks = jnp.where(even, ahead, c)
    lows = [
        (low_span(c + 1 - 2 * side) < low_span(asks)).astype(jnp.int32),
        (low_span(jnp.where(even, c, behind)) < low_span(asks)).astype(jnp.int32),
    ]

    lo, hi = low_place * SPAN, (1 - low_place) * SPAN

    def by_chunk(ref, i, value):
        for r in range(chunks):
            ref[r, pl.ds(i * each, each)] = value[r * each : (r + 1) * each]

    for copy in loads[1:5]:
        copy.wait()
    for i, (raw, place) in enumerate(((raw_q, hi), (raw_g, hi), (raw_q, lo), (raw_g, lo))):
        by_chunk(q_own, i, raw[pl.ds(place, SPAN)])
    for i, (raw, place) in enumerate(((raw_k, lo), (raw_v, lo), (raw_k, hi), (raw_v, hi))):
        by_chunk(kv_own, i, raw[pl.ds(place, SPAN)])

    def remote(src, dst, send, recv, device):
        return pltpu.make_async_remote_copy(
            src_ref=src, dst_ref=dst, send_sem=send, recv_sem=recv, device_id=device, device_id_type=MESH
        )

    order = [lax.rem(h + step, chunks) for step in range(1, chunks + 1)]
    kv_copy = remote(kv_own, kv_mate, kv_sem.at[0], kv_sem.at[1], mate)
    q_copies = [
        remote(q_own.at[j], q_far[j], far_sem.at[0, j], far_sem.at[1, j], {"ctx": behind}) for j in range(chunks)
    ]
    kv_copies = [
        remote(kv_own.at[order[j]], kv_far[j], far_sem.at[0, j], far_sem.at[1, j], {"ctx": ahead})
        for j in range(chunks)
    ]
    row_copies = [
        remote(own, far, row_sem.at[0, i], row_sem.at[1, i], {"ctx": behind})
        for i, (own, far) in enumerate(((norm_own, norm_far), (delta_own, delta_far)))
    ]
    dq_copies = [
        remote(next_out.at[j], dq_part[j], dq_sem.at[0, j], dq_sem.at[1, j], {"ctx": ahead}) for j in range(chunks)
    ]
    back_copies = [
        remote(back_out.at[j], back_part[j], back_sem.at[0, j], back_sem.at[1, j], {"ctx": behind})
        for j in range(chunks)
    ]
    mate_copy = remote(mate_out, mate_part, mate_sem.at[0], mate_sem.at[1], mate)
    starts_line = jnp.logical_and(even, start_of_line)

    def send_chunk(j):
        pl.when(odd)(kv_copies[j].start)
        pl.when(wants_behind)(q_copies[j].start)

    send_chunk(0)
    kv_copy.start()

    for copy in loads[5:]:
        copy.wait()
    for i, place in enumerate((hi, lo)):
        norm_own[:, pl.ds(i * SPAN, SPAN)] = raw_norm[:, pl.ds(place, SPAN)] * LOG2E
        product = raw_g[pl.ds(place, SPAN)].astype(F32) * raw_o[pl.ds(place, SPAN)].astype(F32)
        delta_own[:, pl.ds(i * SPAN, SPAN)] = jnp.sum(product.T, axis=0, keepdims=True)

    def send_rows():
        for copy in row_copies:
            copy.start()

    pl.when(wants_behind)(send_rows)

    def either(a, b):
        return a + b - 2 * a * b

    def at(i, size):
        return pl.ds(i * size, size)

    def whole(ref, i):
        return ref[:, at(i, each)].reshape(SPAN, DIM)

    def block(qpart, kv, kvpart, diagonal=False):
        return tile(
            whole(q_own, 2 * qpart),
            whole(q_own, 2 * qpart + 1),
            norm_own[:, at(qpart, SPAN)],
            delta_own[:, at(qpart, SPAN)],
            whole(kv, 2 * kvpart),
            whole(kv, 2 * kvpart + 1),
            diagonal,
        )

    top, bottom = pl.ds(0, SPAN), pl.ds(SPAN, SPAN)

    dq, dk, dv = block(0, kv_own, 0)
    dq_acc[top] = dq
    dk_acc[0, top] = dk
    dv_acc[0, top] = dv
    send_chunk(1)
    dq, dk, dv = block(1, kv_own, 0, True)
    dq_acc[bottom] = dq
    dk_acc[0, top] += dk
    dv_acc[0, top] += dv
    send_chunk(2)
    dq, dk, dv = block(0, kv_own, 1, True)
    dq_acc[top] += dq
    dk_acc[0, bottom] = dk
    dv_acc[0, bottom] = dv
    send_chunk(3)

    @pl.when(jnp.logical_and(is_even_place, wants_behind))
    def _():
        pl.semaphore_wait(hello.at[0], 1)

    @pl.when(is_even_place)
    def _():
        pl.semaphore_wait(barrier, heads - 1)
        tell_heads(relay)

    def hear_behind():
        pl.semaphore_wait(hello.at[1], 1)
        q_copies[0].start()
        send_rows()
        q_copies[1].start()

    def tell_ahead():
        @pl.when(is_even_place)
        def _():
            pl.semaphore_wait(relay, heads - 1)
            tell(plane, ctx=ahead)

    for ref in (dq_end, dk_end, dv_end):
        for pair in range(2):
            ref[pair, bottom] = jnp.zeros((SPAN, DIM), F32)

    def if_low(pair, part, end, on=1):
        return end[pair, at(1 - on * either(lows[pair], part), SPAN)]

    def split(pair, value):
        is_low = jnp.full(value.shape, lows[pair], jnp.int32) == 1
        return jnp.where(is_low, value, 0.0), jnp.where(is_low, 0.0, value)

    def send_mate():
        for part in range(2):
            for i, (acc, end, factor) in enumerate(((dk_acc, dk_end, SCALE), (dv_acc, dv_end, 1.0))):
                value = if_low(0, part, end)
                if part == 0:
                    value += acc[1, top]
                mate_out[pl.ds(part * TOK + i * SPAN, SPAN)] = (value * factor).astype(BF16)
        mate_copy.start()

    def add(ref, index, value, first):
        ref[index] = value if first else ref[index] + value

    @pl.when(even)
    def _():
        kv_copy.wait_recv()
        for copy in row_copies:
            copy.wait_recv()
        tell_ahead()
        for j in range(chunks):
            if j == 2:
                pl.when(starts_line)(hear_behind)
            if j == 2 + 1:
                pl.when(starts_line)(q_copies[2].start)
            q_copies[j].wait_recv()
            q = q_far[j]
            dq_hi = dq_lo = 0.0
            for pair, kv, slot in ((0, kv_mate, 1), (1, kv_own, 0)):
                row = pl.ds(j * each, each)
                dq, dk, dv = tile(
                    q[at(0, each)], q[at(1, each)], norm_far[:, row], delta_far[:, row], whole(kv, 0), whole(kv, 1)
                )
                dq_hi += dq
                add(dk_acc, (slot, top), dk, j == 0 and slot == 1)
                add(dv_acc, (slot, top), dv, j == 0 and slot == 1)
                is_low = lows[pair]
                row = pl.ds(is_low * SPAN + j * each, each)
                dq, dk, dv = tile(
                    q[at(2 * is_low, each)],
                    q[at(2 * is_low + 1, each)],
                    norm_far[:, row],
                    delta_far[:, row],
                    whole(kv, 2 * (1 - is_low)),
                    whole(kv, 2 * (1 - is_low) + 1),
                )
                to_lo, to_hi = split(pair, dq)
                dq_lo += to_lo
                dq_hi += to_hi
                add(dk_end, (pair, top), dk, j == 0)
                add(dv_end, (pair, top), dv, j == 0)
            next_out[j, at(0, each)] = (dq_hi * SCALE).astype(BF16)
            next_out[j, at(1, each)] = (dq_lo * SCALE).astype(BF16)
            dq_copies[j].start()
        pl.when(starts_line)(q_copies[3].start)
        send_mate()

    @pl.when(odd)
    def _():
        kv_copy.wait_recv()
        dq, dk, dv = block(0, kv_mate, 0)
        dq_acc[top] += dq
        dk_acc[1, top] = dk
        dv_acc[1, top] = dv
        dq, dk, dv = block(lows[0], kv_mate, 1 - lows[0])
        dq_end[0, top] = dq
        dk_end[0, top] = dk
        dv_end[0, top] = dv
        send_mate()
        tell_ahead()

    low_of = [low_place, 1 - low_place]

    def visit_behind():
        @pl.when(is_even_place)
        def _():
            pl.semaphore_wait(hello.at[1], 1)

        is_low = lows[1]
        for j in range(chunks):
            kv_copies[j].wait_recv()
            kv = kv_far[j]
            dq, dk, dv = tile(
                whole(q_own, 0), whole(q_own, 1), norm_own[:, top], delta_own[:, top], kv[at(0, each)], kv[at(1, each)]
            )
            dq_acc[top] += dq
            dq, dk_end_j, dv_end_j = tile(
                whole(q_own, 2 * is_low),
                whole(q_own, 2 * is_low + 1),
                norm_own[:, at(is_low, SPAN)],
                delta_own[:, at(is_low, SPAN)],
                kv[at(2 * (1 - is_low), each)],
                kv[at(2 * (1 - is_low) + 1, each)],
            )
            add(dq_end, (1, top), dq, j == 0)
            for i, (value, end, factor) in enumerate(((dk, dk_end_j, SCALE), (dv, dv_end_j, 1.0))):
                to_lo, to_hi = split(1, end)
                back_out[j, at(i, each)] = ((value + to_lo) * factor).astype(BF16)
                back_out[j, at(2 + i, each)] = (to_hi * factor).astype(BF16)
            back_copies[j].start()
        for p in range(2):
            value = dq_acc[at(1 - low_of[p], SPAN)]
            value += if_low(0, low_of[p], dq_end) + if_low(1, low_of[p], dq_end)
            dq_out[pl.ds(p * SPAN, SPAN)] = (value * SCALE).astype(BF16)

    pl.when(jnp.logical_and(odd, jnp.logical_not(start_of_line)))(visit_behind)

    mate_copy.wait_recv()

    @pl.when(is_odd_place)
    def _():
        pl.semaphore_wait(plane, 1)

    def own_copy(to):
        return remote(own_out.at[to], own_part.at[h], own_send.at[to], own_recv.at[h], {"head": to})

    for j, r in enumerate(order):
        pl.when(odd)(back_copies[j].wait_recv)
        for p in range(2):
            part = low_of[p]
            to = p * chunks + r
            row = r * each

            def rows_of(i):
                return pl.ds(i * SPAN + row, each)

            halves = []
            for i, (acc, end, factor) in enumerate(((dk_acc, dk_end, SCALE), (dv_acc, dv_end, 1.0))):
                more = end[1, rows_of(1 - (1 - side) * either(lows[1], part))]
                value = (acc[0, rows_of(part)] + more) * factor
                halves.append(value + mate_part[rows_of(2 * part + i)].astype(F32))

            @pl.when(even)
            def _():
                for i in range(2):
                    own_out[to, at(i, each)] = halves[i].astype(BF16)

            @pl.when(odd)
            def _():
                for i in range(2):
                    back = back_part[j][at(2 * part + i, each)].astype(F32)
                    own_out[to, at(i, each)] = (halves[i] + back).astype(BF16)

            if j < chunks - 1:
                own_copy(to).start()
            else:
                pl.when(to != h)(own_copy(to).start)
    own_part[h] = own_out[h]

    pl.when(jnp.logical_and(odd, start_of_line))(visit_behind)

    def finish_queries():
        for j in range(chunks):
            dq_copies[j].wait_recv()
            for p in range(2):
                place = 1 - low_of[p]
                own = dq_acc[pl.ds(place * SPAN + j * each, each)] * SCALE
                far = dq_part[j][at(place, each)].astype(F32)
                dq_out[pl.ds(p * SPAN + j * each, each)] = (own + far).astype(BF16)

    pl.when(wants_behind)(finish_queries)

    for step in range(1, heads):
        sender = lax.rem(h + step, heads)
        remote(own_out.at[sender], own_part.at[sender], own_send.at[sender], own_recv.at[sender], mate).wait_recv()
    total = own_part[0].astype(F32)
    for i in range(1, heads):
        total += own_part[i].astype(F32)
    dkv_out[...] = total.astype(BF16)
    pl.when(starts_line)(finish_queries)

    kv_copy.wait_send()
    mate_copy.wait_send()
    for step in range(1, heads):
        own_copy(lax.rem(h + step, heads)).wait_send()

    @pl.when(even)
    def _():
        for copy in (*row_copies, *q_copies, *dq_copies):
            copy.wait_send()

    @pl.when(odd)
    def _():
        for copy in (*kv_copies, *back_copies):
            copy.wait_send()


def local(queries, keys, values, outputs, out_grad, log_norm, span_ids):
    holders, heads = lax.axis_size("ctx"), lax.axis_size("head")
    each, chunks = TOK // heads, heads // 2
    flat = lambda a: a.reshape(TOK, DIM)
    body = lambda *refs: kernel(holders, heads, *refs)
    dma = pltpu.SemaphoreType.DMA
    dq, dkv = pl.pallas_call(
        body,
        out_shape=[
            pltpu.VMEM((TOK, DIM), BF16),
            pltpu.VMEM((2 * each, DIM), BF16),
        ],
        in_specs=[
            *[pl.BlockSpec(memory_space=pltpu.HBM)] * 7,
        ],
        out_specs=[pl.BlockSpec(memory_space=pltpu.VMEM)] * 2,
        scratch_shapes=[
            pltpu.SMEM((2 * holders,), jnp.int32),
            pltpu.VMEM((1, TOK), F32),
            *[pltpu.VMEM((TOK, DIM), BF16)] * 5,
            *[pltpu.VMEM((chunks, 4 * each, DIM), BF16)] * 3,
            *[pltpu.VMEM((4 * each, DIM), BF16)] * (2 * chunks),
            *[pltpu.VMEM((2 * each, DIM), BF16)] * chunks,
            *[pltpu.VMEM((4 * each, DIM), BF16)] * chunks,
            *[pltpu.VMEM((1, TOK), F32)] * 4,
            pltpu.VMEM((TOK, DIM), F32),
            *[pltpu.VMEM((2, TOK, DIM), F32)] * 5,
            pltpu.VMEM((2 * TOK, DIM), BF16),
            pltpu.VMEM((2 * TOK, DIM), BF16),
            pltpu.VMEM((chunks, 2 * each, DIM), BF16),
            pltpu.VMEM((chunks, 4 * each, DIM), BF16),
            pltpu.VMEM((heads, 2 * each, DIM), BF16),
            pltpu.VMEM((heads, 2 * each, DIM), BF16),
            dma((7,)),
            dma((2,)),
            dma((2,)),
            dma((2, chunks)),
            dma((2, 2)),
            dma((2, chunks)),
            dma((2, chunks)),
            dma((heads,)),
            dma((heads,)),
            pltpu.SemaphoreType.REGULAR((2,)),
            pltpu.SemaphoreType.REGULAR,
            pltpu.SemaphoreType.REGULAR,
        ],
        compiler_params=pltpu.CompilerParams(
            collective_id=0, has_side_effects=True, vmem_limit_bytes=VMEM_GRANT
        ),
    )(
        span_ids,
        flat(queries),
        flat(out_grad),
        flat(outputs),
        keys,
        values,
        log_norm,
    )
    return dq.reshape(queries.shape), dkv[:each], dkv[each:]


def solution(mesh):
    in_specs = (
        P("ctx", "head", None),
        P("ctx", None),
        P("ctx", None),
        P("ctx", "head", None),
        P("ctx", "head", None),
        P("head", "ctx"),
        P(),
    )
    out_specs = (P("ctx", "head", None), P(("ctx", "head"), None), P(("ctx", "head"), None))
    return jax.shard_map(local, mesh=mesh, in_specs=in_specs, out_specs=out_specs, check_vma=False)
```

```python
import jax
import jax.numpy as jnp
from jax import lax
from jax.experimental import pallas as pl
from jax.experimental.pallas import tpu as pltpu
from jax.sharding import PartitionSpec as P

MESH = pl.DeviceIdType.MESH
F32 = jnp.float32
BF16 = jnp.bfloat16
LOG2E = 1.4426950408889634
NT = (((1,), (1,)), ((), ()))
TN = (((0,), (0,)), ((), ()))
SPAN = 512
LINE = 16
VMEM_GRANT = 63 * 1024 * 1024
TOK = 2 * SPAN
DIM = 128
SCALE = DIM ** -0.5


def tile(q, g, norm, delta, k, v, diagonal=False):
    score = lax.dot_general(k, q, NT, preferred_element_type=F32)
    prob = jnp.exp2(score * (SCALE * LOG2E) - norm)
    if diagonal:
        rows = lax.broadcasted_iota(jnp.int32, score.shape, 0)
        prob = jnp.where(rows <= lax.broadcasted_iota(jnp.int32, score.shape, 1), prob, 0.0)
    dprob = lax.dot_general(v, g, NT, preferred_element_type=F32)
    dscore = (prob * (dprob - delta)).astype(BF16)
    dv = jnp.dot(prob.astype(BF16), g, preferred_element_type=F32)
    dk = jnp.dot(dscore, q, preferred_element_type=F32)
    dq = lax.dot_general(dscore, k, TN, preferred_element_type=F32)
    return dq, dk, dv


def kernel(
    holders, heads, span_in, q_in, g_in, o_in, k_in, v_in, norm_in, dq_out, dkv_out,
    span_ref, raw_norm, raw_q, raw_g, raw_k, raw_v, raw_o, q_own, kv_own, kv_mate,
    *rest,
):
    chunks = heads // 2
    q_far, kv_far, dq_part, back_part, mate_part = (rest[i * chunks : (i + 1) * chunks] for i in range(5))
    (
        norm_own, norm_far, delta_own, delta_far, dq_acc, dk_acc, dv_acc, dq_end, dk_end, dv_end,
        mate_out, next_out, back_out, own_out, own_part,
        load_sem, kv_sem, mate_sem, far_sem, row_sem, dq_sem, back_sem, own_send, own_recv,
        hello, relay, plane,
    ) = rest[5 * chunks :]
    each = TOK // heads
    c = lax.axis_index("ctx")
    h = lax.axis_index("head")
    side = lax.rem(c, 2)
    even, odd = side == 0, side == 1
    mate = {"ctx": c + 1 - 2 * side}
    ahead = lax.rem(c + 2, holders)
    behind = lax.rem(c + holders - 2, holders)

    place_in_line = lax.rem(lax.div(c, 2), LINE)
    start_of_line, end_of_line = place_in_line == 0, place_in_line == LINE - 1
    is_odd_place = lax.rem(place_in_line, 2) == 1
    is_even_place = lax.rem(place_in_line, 2) == 0

    loads = [
        pltpu.make_async_copy(ref, raw, load_sem.at[i])
        for i, (ref, raw) in enumerate(
            (
                (span_in, span_ref), (k_in, raw_k), (v_in, raw_v), (q_in, raw_q), (g_in, raw_g),
                (norm_in, raw_norm), (o_in, raw_o),
            )
        )
    ]
    for copy in loads:
        copy.start()

    barrier = pltpu.get_barrier_semaphore()

    def tell(sem, **device):
        pl.semaphore_signal(sem, inc=1, device_id=device, device_id_type=MESH)

    def tell_heads(sem):
        for step in range(1, heads):
            tell(sem, head=lax.rem(h + step, heads))

    @pl.when(is_even_place)
    def _():
        for holder in (ahead, behind):
            tell(barrier, ctx=holder)
            tell(barrier, ctx=holder + 1 - 2 * side)
        tell_heads(barrier)

    wants_behind = jnp.logical_and(even, jnp.logical_not(start_of_line))

    @pl.when(jnp.logical_and(is_even_place, wants_behind))
    def _():
        pl.semaphore_wait(hello.at[1], 1)

    @pl.when(jnp.logical_and(is_even_place, jnp.logical_not(wants_behind)))
    def _():
        pl.semaphore_wait(hello.at[0], 1)

    @pl.when(is_odd_place)
    def _():
        tell(barrier, **mate)
        pl.semaphore_wait(barrier, 5)
        tell(hello.at[0], ctx=behind)
        tell(hello.at[1], ctx=ahead)

    loads[0].wait()

    def first(holder):
        return span_ref[2 * holder]

    def second(holder):
        return span_ref[2 * holder + 1]

    def low_span(holder):
        return jnp.minimum(first(holder), second(holder))

    def late(holder):
        return (first(holder) > second(holder)).astype(jnp.int32)

    low_place = late(c)
    asks = jnp.where(even, ahead, c)
    lows = [
        (low_span(c + 1 - 2 * side) < low_span(asks)).astype(jnp.int32),
        (low_span(jnp.where(even, c, behind)) < low_span(asks)).astype(jnp.int32),
    ]

    lo, hi = low_place * SPAN, (1 - low_place) * SPAN

    def by_chunk(ref, i, value):
        for r in range(chunks):
            ref[r, pl.ds(i * each, each)] = value[r * each : (r + 1) * each]

    for copy in loads[1:5]:
        copy.wait()
    for i, (raw, place) in enumerate(((raw_q, hi), (raw_g, hi), (raw_q, lo), (raw_g, lo))):
        by_chunk(q_own, i, raw[pl.ds(place, SPAN)])
    for i, (raw, place) in enumerate(((raw_k, lo), (raw_v, lo), (raw_k, hi), (raw_v, hi))):
        by_chunk(kv_own, i, raw[pl.ds(place, SPAN)])

    def remote(src, dst, send, recv, device):
        return pltpu.make_async_remote_copy(
            src_ref=src, dst_ref=dst, send_sem=send, recv_sem=recv, device_id=device, device_id_type=MESH
        )

    order = [lax.rem(h + step, chunks) for step in range(1, chunks + 1)]
    kv_copy = remote(kv_own, kv_mate, kv_sem.at[0], kv_sem.at[1], mate)
    q_copies = [
        remote(q_own.at[j], q_far[j], far_sem.at[0, j], far_sem.at[1, j], {"ctx": behind}) for j in range(chunks)
    ]
    kv_copies = [
        remote(kv_own.at[order[j]], kv_far[j], far_sem.at[0, j], far_sem.at[1, j], {"ctx": ahead})
        for j in range(chunks)
    ]
    row_copies = [
        remote(own, far, row_sem.at[0, i], row_sem.at[1, i], {"ctx": behind})
        for i, (own, far) in enumerate(((norm_own, norm_far), (delta_own, delta_far)))
    ]
    dq_copies = [
        remote(next_out.at[j], dq_part[j], dq_sem.at[0, j], dq_sem.at[1, j], {"ctx": ahead}) for j in range(chunks)
    ]
    back_copies = [
        remote(back_out.at[j], back_part[j], back_sem.at[0, j], back_sem.at[1, j], {"ctx": behind})
        for j in range(chunks)
    ]
    mate_copies = [
        remote(mate_out.at[j], mate_part[j], mate_sem.at[0, j], mate_sem.at[1, j], mate) for j in range(chunks)
    ]
    starts_line = jnp.logical_and(even, start_of_line)

    def send_chunk(j):
        pl.when(odd)(kv_copies[j].start)
        pl.when(wants_behind)(q_copies[j].start)

    send_chunk(0)
    kv_copy.start()

    for copy in loads[5:]:
        copy.wait()
    for i, place in enumerate((hi, lo)):
        norm_own[:, pl.ds(i * SPAN, SPAN)] = raw_norm[:, pl.ds(place, SPAN)] * LOG2E
        product = raw_g[pl.ds(place, SPAN)].astype(F32) * raw_o[pl.ds(place, SPAN)].astype(F32)
        delta_own[:, pl.ds(i * SPAN, SPAN)] = jnp.sum(product.T, axis=0, keepdims=True)

    def send_rows():
        for copy in row_copies:
            copy.start()

    pl.when(wants_behind)(send_rows)

    def either(a, b):
        return a + b - 2 * a * b

    def at(i, size):
        return pl.ds(i * size, size)

    def whole(ref, i):
        return ref[:, at(i, each)].reshape(SPAN, DIM)

    def block(qpart, kv, kvpart, diagonal=False):
        return tile(
            whole(q_own, 2 * qpart),
            whole(q_own, 2 * qpart + 1),
            norm_own[:, at(qpart, SPAN)],
            delta_own[:, at(qpart, SPAN)],
            whole(kv, 2 * kvpart),
            whole(kv, 2 * kvpart + 1),
            diagonal,
        )

    top, bottom = pl.ds(0, SPAN), pl.ds(SPAN, SPAN)

    dq, dk, dv = block(0, kv_own, 0)
    dq_acc[top] = dq
    dk_acc[0, top] = dk
    dv_acc[0, top] = dv
    send_chunk(1)
    dq, dk, dv = block(1, kv_own, 0, True)
    dq_acc[bottom] = dq
    dk_acc[0, top] += dk
    dv_acc[0, top] += dv
    send_chunk(2)
    dq, dk, dv = block(0, kv_own, 1, True)
    dq_acc[top] += dq
    dk_acc[0, bottom] = dk
    dv_acc[0, bottom] = dv
    send_chunk(3)

    @pl.when(jnp.logical_and(is_even_place, wants_behind))
    def _():
        pl.semaphore_wait(hello.at[0], 1)

    @pl.when(is_even_place)
    def _():
        pl.semaphore_wait(barrier, heads - 1)
        tell_heads(relay)

    def hear_behind():
        pl.semaphore_wait(hello.at[1], 1)
        q_copies[0].start()
        send_rows()
        q_copies[1].start()

    def tell_ahead():
        @pl.when(is_even_place)
        def _():
            pl.semaphore_wait(relay, heads - 1)
            tell(plane, ctx=ahead)

    for ref in (dq_end, dk_end, dv_end):
        for pair in range(2):
            ref[pair, bottom] = jnp.zeros((SPAN, DIM), F32)

    def if_low(pair, part, end, on=1):
        return end[pair, at(1 - on * either(lows[pair], part), SPAN)]

    def split(pair, value):
        is_low = jnp.full(value.shape, lows[pair], jnp.int32) == 1
        return jnp.where(is_low, value, 0.0), jnp.where(is_low, 0.0, value)

    def send_mate():
        for j, r in enumerate(order):
            for part in range(2):
                for i, (acc, end, factor) in enumerate(((dk_acc, dk_end, SCALE), (dv_acc, dv_end, 1.0))):
                    value = end[0, pl.ds((1 - either(lows[0], part)) * SPAN + r * each, each)]
                    if part == 0:
                        value += acc[1, pl.ds(r * each, each)]
                    mate_out[j, at(2 * part + i, each)] = (value * factor).astype(BF16)
            mate_copies[j].start()

    def add(ref, index, value, first):
        ref[index] = value if first else ref[index] + value

    @pl.when(even)
    def _():
        kv_copy.wait_recv()
        for copy in row_copies:
            copy.wait_recv()
        tell_ahead()
        for j in range(chunks):
            if j == 2:
                pl.when(starts_line)(hear_behind)
            if j == 2 + 1:
                pl.when(starts_line)(q_copies[2].start)
            q_copies[j].wait_recv()
            q = q_far[j]
            dq_hi = dq_lo = 0.0
            for pair, kv, slot in ((0, kv_mate, 1), (1, kv_own, 0)):
                row = pl.ds(j * each, each)
                dq, dk, dv = tile(
                    q[at(0, each)], q[at(1, each)], norm_far[:, row], delta_far[:, row], whole(kv, 0), whole(kv, 1)
                )
                dq_hi += dq
                add(dk_acc, (slot, top), dk, j == 0 and slot == 1)
                add(dv_acc, (slot, top), dv, j == 0 and slot == 1)
                is_low = lows[pair]
                row = pl.ds(is_low * SPAN + j * each, each)
                dq, dk, dv = tile(
                    q[at(2 * is_low, each)],
                    q[at(2 * is_low + 1, each)],
                    norm_far[:, row],
                    delta_far[:, row],
                    whole(kv, 2 * (1 - is_low)),
                    whole(kv, 2 * (1 - is_low) + 1),
                )
                to_lo, to_hi = split(pair, dq)
                dq_lo += to_lo
                dq_hi += to_hi
                add(dk_end, (pair, top), dk, j == 0)
                add(dv_end, (pair, top), dv, j == 0)
            next_out[j, at(0, each)] = (dq_hi * SCALE).astype(BF16)
            next_out[j, at(1, each)] = (dq_lo * SCALE).astype(BF16)
            dq_copies[j].start()
        pl.when(starts_line)(q_copies[3].start)
        send_mate()

    @pl.when(odd)
    def _():
        kv_copy.wait_recv()
        dq, dk, dv = block(0, kv_mate, 0)
        dq_acc[top] += dq
        dk_acc[1, top] = dk
        dv_acc[1, top] = dv
        dq, dk, dv = block(lows[0], kv_mate, 1 - lows[0])
        dq_end[0, top] = dq
        dk_end[0, top] = dk
        dv_end[0, top] = dv
        send_mate()
        tell_ahead()

    low_of = [low_place, 1 - low_place]

    def visit_behind():
        @pl.when(is_even_place)
        def _():
            pl.semaphore_wait(hello.at[1], 1)

        is_low = lows[1]
        for j in range(chunks):
            kv_copies[j].wait_recv()
            kv = kv_far[j]
            dq, dk, dv = tile(
                whole(q_own, 0), whole(q_own, 1), norm_own[:, top], delta_own[:, top], kv[at(0, each)], kv[at(1, each)]
            )
            dq_acc[top] += dq
            dq, dk_end_j, dv_end_j = tile(
                whole(q_own, 2 * is_low),
                whole(q_own, 2 * is_low + 1),
                norm_own[:, at(is_low, SPAN)],
                delta_own[:, at(is_low, SPAN)],
                kv[at(2 * (1 - is_low), each)],
                kv[at(2 * (1 - is_low) + 1, each)],
            )
            add(dq_end, (1, top), dq, j == 0)
            for i, (value, end, factor) in enumerate(((dk, dk_end_j, SCALE), (dv, dv_end_j, 1.0))):
                to_lo, to_hi = split(1, end)
                back_out[j, at(i, each)] = ((value + to_lo) * factor).astype(BF16)
                back_out[j, at(2 + i, each)] = (to_hi * factor).astype(BF16)
            back_copies[j].start()
        for p in range(2):
            value = dq_acc[at(1 - low_of[p], SPAN)]
            value += if_low(0, low_of[p], dq_end) + if_low(1, low_of[p], dq_end)
            dq_out[pl.ds(p * SPAN, SPAN)] = (value * SCALE).astype(BF16)

    pl.when(jnp.logical_and(odd, jnp.logical_not(start_of_line)))(visit_behind)

    @pl.when(is_odd_place)
    def _():
        pl.semaphore_wait(plane, 1)

    def own_copy(to):
        return remote(own_out.at[to], own_part.at[h], own_send.at[to], own_recv.at[h], {"head": to})

    for j, r in enumerate(order):
        mate_copies[j].wait_recv()
        pl.when(odd)(back_copies[j].wait_recv)
        for p in range(2):
            part = low_of[p]
            to = p * chunks + r
            row = r * each

            def rows_of(i):
                return pl.ds(i * SPAN + row, each)

            halves = []
            for i, (acc, end, factor) in enumerate(((dk_acc, dk_end, SCALE), (dv_acc, dv_end, 1.0))):
                more = end[1, rows_of(1 - (1 - side) * either(lows[1], part))]
                value = (acc[0, rows_of(part)] + more) * factor
                halves.append(value + mate_part[j][at(2 * part + i, each)].astype(F32))

            @pl.when(even)
            def _():
                for i in range(2):
                    own_out[to, at(i, each)] = halves[i].astype(BF16)

            @pl.when(odd)
            def _():
                for i in range(2):
                    back = back_part[j][at(2 * part + i, each)].astype(F32)
                    own_out[to, at(i, each)] = (halves[i] + back).astype(BF16)

            if j < chunks - 1:
                own_copy(to).start()
            else:
                pl.when(to != h)(own_copy(to).start)
    own_part[h] = own_out[h]

    pl.when(jnp.logical_and(odd, start_of_line))(visit_behind)

    def finish_queries():
        for j in range(chunks):
            dq_copies[j].wait_recv()
            for p in range(2):
                place = 1 - low_of[p]
                own = dq_acc[pl.ds(place * SPAN + j * each, each)] * SCALE
                far = dq_part[j][at(place, each)].astype(F32)
                dq_out[pl.ds(p * SPAN + j * each, each)] = (own + far).astype(BF16)

    pl.when(wants_behind)(finish_queries)

    for step in range(1, heads):
        sender = lax.rem(h + step, heads)
        remote(own_out.at[sender], own_part.at[sender], own_send.at[sender], own_recv.at[sender], mate).wait_recv()
    total = own_part[0].astype(F32)
    for i in range(1, heads):
        total += own_part[i].astype(F32)
    dkv_out[...] = total.astype(BF16)
    pl.when(starts_line)(finish_queries)

    kv_copy.wait_send()
    for copy in mate_copies:
        copy.wait_send()
    for step in range(1, heads):
        own_copy(lax.rem(h + step, heads)).wait_send()

    @pl.when(even)
    def _():
        for copy in (*row_copies, *q_copies, *dq_copies):
            copy.wait_send()

    @pl.when(odd)
    def _():
        for copy in (*kv_copies, *back_copies):
            copy.wait_send()


def local(queries, keys, values, outputs, out_grad, log_norm, span_ids):
    holders, heads = lax.axis_size("ctx"), lax.axis_size("head")
    each, chunks = TOK // heads, heads // 2
    flat = lambda a: a.reshape(TOK, DIM)
    body = lambda *refs: kernel(holders, heads, *refs)
    dma = pltpu.SemaphoreType.DMA
    dq, dkv = pl.pallas_call(
        body,
        out_shape=[
            pltpu.VMEM((TOK, DIM), BF16),
            pltpu.VMEM((2 * each, DIM), BF16),
        ],
        in_specs=[
            *[pl.BlockSpec(memory_space=pltpu.HBM)] * 7,
        ],
        out_specs=[pl.BlockSpec(memory_space=pltpu.VMEM)] * 2,
        scratch_shapes=[
            pltpu.SMEM((2 * holders,), jnp.int32),
            pltpu.VMEM((1, TOK), F32),
            *[pltpu.VMEM((TOK, DIM), BF16)] * 5,
            *[pltpu.VMEM((chunks, 4 * each, DIM), BF16)] * 3,
            *[pltpu.VMEM((4 * each, DIM), BF16)] * (2 * chunks),
            *[pltpu.VMEM((2 * each, DIM), BF16)] * chunks,
            *[pltpu.VMEM((4 * each, DIM), BF16)] * (2 * chunks),
            *[pltpu.VMEM((1, TOK), F32)] * 4,
            pltpu.VMEM((TOK, DIM), F32),
            *[pltpu.VMEM((2, TOK, DIM), F32)] * 5,
            pltpu.VMEM((chunks, 4 * each, DIM), BF16),
            pltpu.VMEM((chunks, 2 * each, DIM), BF16),
            pltpu.VMEM((chunks, 4 * each, DIM), BF16),
            pltpu.VMEM((heads, 2 * each, DIM), BF16),
            pltpu.VMEM((heads, 2 * each, DIM), BF16),
            dma((7,)),
            dma((2,)),
            dma((2, chunks)),
            dma((2, chunks)),
            dma((2, 2)),
            dma((2, chunks)),
            dma((2, chunks)),
            dma((heads,)),
            dma((heads,)),
            pltpu.SemaphoreType.REGULAR((2,)),
            pltpu.SemaphoreType.REGULAR,
            pltpu.SemaphoreType.REGULAR,
        ],
        compiler_params=pltpu.CompilerParams(
            collective_id=0, has_side_effects=True, vmem_limit_bytes=VMEM_GRANT
        ),
    )(
        span_ids,
        flat(queries),
        flat(out_grad),
        flat(outputs),
        keys,
        values,
        log_norm,
    )
    return dq.reshape(queries.shape), dkv[:each], dkv[each:]


def solution(mesh):
    in_specs = (
        P("ctx", "head", None),
        P("ctx", None),
        P("ctx", None),
        P("ctx", "head", None),
        P("ctx", "head", None),
        P("head", "ctx"),
        P(),
    )
    out_specs = (P("ctx", "head", None), P(("ctx", "head"), None), P(("ctx", "head"), None))
    return jax.shard_map(local, mesh=mesh, in_specs=in_specs, out_specs=out_specs, check_vma=False)
```
